128 devices in a mesh: grid: 8 (over y, core), prow: 4 (over z), pcol: 4 (over x).
Axes of the slice: x: 4, y: 4, z: 4, core: 2. Of those that a mesh axis runs over, the one named last changes fastest.
Arguments:
- updates: bfloat16 [8, 4096, 4096], P('grid', ('prow', 'pcol')), may hold values from -0.09375 to 0.09375
- row_mask: int32 [8, 16], P('grid'), may hold values 0 or 1
- base: float32 [4096, 4, 1024], P('prow', 'pcol', 'grid'), may hold values from -1 to 4, as said below
Outputs:
- schur: float32 [4096, 4, 1024], P('prow', 'pcol', 'grid')
- panels: float32 [4096, 512], P('prow')
The draws below stay inside these ranges and needn't reach their ends.
Inputs may be any that keep to these rules, and one draw needn't show every extreme that they name: Read through the column layout, base is a symmetric, strictly diagonally dominant matrix with a positive diagonal.
All inputs are finite; a program needn't handle non-finite values. No bound on the sum of `row_mask` on one device may be relied on, other than what follows from the above.
Results may differ from the reference program's by a relative error of at most 0.0003.
Values may be sent and summed in bfloat16 or wider, within the bound.
A program may use at most 128 MiB of HBM per device.

```python
import jax
import jax.numpy as jnp
from jax import lax

TILE = 256
BLOCK = 256
K = 4096
PANELS = 2
M = 4096
TILES = 16
N_GRID = 8
N_PROW = 4
N_PCOL = 4


def draw_base(key, part):
    key = jax.random.fold_in(key, 7)
    first_key = jax.random.fold_in(key, 0)
    third_key = jax.random.fold_in(key, 2)
    raw = jax.random.uniform(first_key, (M, M), jnp.float32, -1.0, 1.0)
    side = (raw + raw.T) * (0.25 / M)
    lift = jax.random.uniform(third_key, (M,), jnp.float32, 0.5, 2.0)
    same = jnp.arange(M)[:, None] == jnp.arange(M)[None, :]
    matrix = jnp.where(same, 0.5 + lift[:, None], side)
    grouped = matrix.reshape(M, N_PROW, N_PCOL, BLOCK)
    return jnp.transpose(grouped, (0, 2, 1, 3)).reshape(M, N_PCOL, N_PROW * BLOCK).astype(jnp.float32)


def set_ends(entries, rng, smallest, largest):
    place = [jax.random.randint(jax.random.fold_in(rng, axis), (), 0, length) for axis, length in enumerate(entries.shape)]
    widest = entries.shape.index(max(entries.shape))
    beside = place[:widest] + [(place[widest] + 1) % entries.shape[widest]] + place[widest + 1:]
    return entries.at[tuple(place)].set(smallest).at[tuple(beside)].set(largest)


def level_of(rng, dims, cuts, smallest, largest):
    factor_of = 1.0
    for axis_at, shards_of in cuts:
        heights = jax.random.uniform(jax.random.fold_in(jax.random.fold_in(rng, 6), axis_at), (shards_of,), jnp.float32, smallest / len(cuts), largest / len(cuts))
        factor_of = factor_of * jnp.repeat(jnp.exp(heights), dims[axis_at] // shards_of).reshape((-1,) + (1,) * (len(dims) - 1 - axis_at))
    return factor_of


def noise(stream_key, dims, deviation, bound, cuts=(), held_as=jnp.bfloat16):
    level = level_of(stream_key, dims, cuts, -0.22, 0.18) if cuts else 1.0
    result = jax.random.normal(stream_key, dims, jnp.float32) * deviation * level
    return jnp.minimum(jnp.maximum(result, -bound), bound).astype(held_as)


def setup_inputs(seed: int = 0) -> dict:
    splits = jax.random.split(jax.random.key(seed), 4)
    updates = noise(splits[0], (N_GRID, M, K), K ** -0.5, 0.09375, ((0, 8), (1, 16)))
    row_mask = set_ends((jax.random.randint(splits[1], (N_GRID, TILES), 0, 3) < 2).astype(jnp.int32), jax.random.fold_in(splits[1], 1), 0, 1)
    base = draw_base(jax.random.fold_in(splits[3], 71), 0)
    return dict(updates=updates, row_mask=row_mask, base=base)


def to_matrix(layout):
    rows = layout.shape[0]
    grouped = layout.reshape(rows, N_PCOL, N_PROW, BLOCK)
    return jnp.transpose(grouped, (0, 2, 1, 3)).reshape(rows, rows)

def to_layout(matrix):
    rows = matrix.shape[0]
    grouped = matrix.reshape(rows, N_PROW, N_PCOL, BLOCK)
    return jnp.transpose(grouped, (0, 2, 1, 3)).reshape(rows, N_PCOL, N_PROW * BLOCK)

def right_solve(diag_tile, column):
    factor = jnp.linalg.cholesky(diag_tile)
    half_solved = jax.scipy.linalg.solve_triangular(factor, column.T, lower=True)
    return jax.scipy.linalg.solve_triangular(factor, half_solved, lower=True, trans='T').T

def reference(updates, row_mask, base):

    def add_grid(matrix_sum, pair):
        grid_rows, grid_mask = pair
        expanded = jnp.repeat(grid_mask, TILE)
        masked = jnp.where(expanded[:, None] > 0, grid_rows, jnp.zeros_like(grid_rows))
        product = lax.dot_general(masked.astype(jnp.float32), masked.astype(jnp.float32), (((1,), (1,)), ((), ())), preferred_element_type=jnp.float32)
        return (matrix_sum + product, None)
    matrix_sum, ignored = lax.scan(add_grid, to_matrix(base), (updates, row_mask))
    lower_list = []
    for panel_index in range(PANELS):
        column = matrix_sum[:, panel_index * TILE:(panel_index + 1) * TILE]
        diag_tile = column[panel_index * TILE:(panel_index + 1) * TILE]
        lower_panel = right_solve(diag_tile, column)
        lower_list.append(lower_panel)
        matrix_sum = matrix_sum - jnp.dot(lower_panel, column.T, precision=lax.Precision.HIGHEST)
    return (to_layout(matrix_sum), jnp.concatenate(lower_list, axis=1))
```

```python
import jax
import jax.numpy as jnp
from jax import lax
from jax.experimental import pallas as pl
from jax.experimental.pallas import tpu as pltpu
from jax.sharding import PartitionSpec as P

TILE = 256
HALF = 128
DEPTH = 4096
ROWS = 1024
CHUNK = 64
MESH = pl.DeviceIdType.MESH
HIGHEST = lax.Precision.HIGHEST
OFFSETS = (0, 1, 3, 2)


def wrap(value):
    return lax.rem(value + 4, 4)


class Copies:
    def __init__(self, send_sems, recv_sems):
        self.send_sems, self.recv_sems, self.count = send_sems, recv_sems, 0

    def take(self, number=1):
        first = self.count
        self.count += number
        return first

    def make(self, src, dst, device, index, recv_index=None):
        return pltpu.make_async_remote_copy(
            src_ref=src,
            dst_ref=dst,
            send_sem=self.send_sems.at[index],
            recv_sem=self.recv_sems.at[index if recv_index is None else recv_index],
            device_id=device,
            device_id_type=MESH,
        )


class Spread:
    def __init__(self, copies, step, place, holds, block):
        rows = block.shape[0] // 2
        self.place, self.holds = place, holds
        first = copies.take(4)
        upper, lower = block.at[pl.ds(0, rows)], block.at[pl.ds(rows, rows)]
        self.up = copies.make(block, block, step(1), first)
        self.down = copies.make(block, block, step(-1), first + 1)
        self.up_half = copies.make(upper, upper, step(1), first + 2)
        self.down_half = copies.make(lower, lower, step(-1), first + 3)

    def when(self, place):
        return pl.when(jnp.logical_and(self.holds, self.place == place))

    def start(self):
        @pl.when(jnp.logical_and(self.holds, self.place == 0))
        def _():
            self.up.start()
            self.down.start()

    def forward(self):
        @self.when(1)
        def _():
            self.up.wait_recv()
            self.up_half.start()

        @self.when(3)
        def _():
            self.down.wait_recv()
            self.down_half.start()

    def arrive(self):
        @self.when(2)
        def _():
            self.up_half.wait_recv()
            self.down_half.wait_recv()

    def finish(self):
        @self.when(0)
        def _():
            self.up.wait_send()
            self.down.wait_send()

        @self.when(1)
        def _():
            self.up_half.wait_send()

        @self.when(3)
        def _():
            self.down_half.wait_send()


def gather_kernel(
    u_ref, mask_ref, base_ref, share_ref, panel_ref, diag_ref, mirror_ref,
    tiles, grams, pairs, arrived, arrived_panel, send_sems, recv_sems,
):
    grid = lax.axis_index("grid")
    r = lax.axis_index("prow")
    c = lax.axis_index("pcol")
    y, k = grid // 2, lax.rem(grid, 2)
    copies = Copies(send_sems, recv_sems)
    sibling = {"grid": y * 2 + 1 - k}

    def step_x(d):
        return {"pcol": wrap(c + d)}

    def step_y(d):
        return {"grid": wrap(y + d) * 2 + k}

    def step_z(d):
        return {"prow": wrap(r + d)}

    barrier = pltpu.get_barrier_semaphore()
    others = [step_x(1), step_x(-1), step_z(1), step_z(-1), step_y(1), step_y(-1), step_y(2), sibling]
    for other in others:
        pl.semaphore_signal(barrier, inc=1, device_id=other, device_id_type=MESH)
    pl.semaphore_wait(barrier, len(others))

    keep = mask_ref[0, r * 4 + c] > 0
    first_hop, second_hop = {}, {}
    streams = [(step, d, base_slot) for step, base_slot in ((step_x, 0), (step_z, 3)) for d in (-1, 1)]

    def rows_of(slot, start, size):
        return tiles.at[pl.ds(slot * TILE + start, size)]

    for part in range(TILE // CHUNK):
        start = part * CHUNK
        value = u_ref[pl.ds(start, CHUNK), :]
        tiles[pl.ds(start, CHUNK), :] = jnp.where(keep, value, jnp.zeros_like(value))
        for step, d, base_slot in streams:
            slot = base_slot + (1 if d == -1 else 2)
            copy = copies.make(rows_of(0, start, CHUNK), rows_of(slot, start, CHUNK), step(d), copies.take())
            copy.start()
            first_hop[base_slot, d, part] = copy

    def gram(rows_start, rows, slot, columns_start=0, columns=TILE):
        return lax.dot_general(
            tiles[pl.ds(rows_start, rows), :],
            tiles[pl.ds(slot * TILE + columns_start, columns), :],
            (((1,), (1,)), ((), ())),
            preferred_element_type=jnp.float32,
        )

    for part in range(TILE // CHUNK):
        start = part * CHUNK
        for step, d, base_slot in streams:
            first_hop[base_slot, d, part].wait_recv()
            if part % 2 == (0 if d == 1 else 1):
                slot = base_slot + (1 if d == -1 else 2)
                copy = copies.make(
                    rows_of(slot, start, CHUNK), rows_of(base_slot + 3, start, CHUNK), step(d), copies.take()
                )
                copy.start()
                second_hop[base_slot, part] = copy

    column_slots = (0, 4, 5, 6)

    class Unit:
        def __init__(self, d, e, halves, start=0, rows=TILE):
            self.d, self.e, self.halves, self.start, self.rows = d, e, halves, start, rows
            self.place = pl.ds(d * TILE + start, rows)
            self.q = wrap(r + OFFSETS[e])
            self.i = wrap(c + OFFSETS[d])
            self.is_panel = jnp.logical_and(c < 2, self.q == 0)
            self.target = jnp.where(self.is_panel, self.i, self.q)
            self.pair_index = copies.take()
            self.send_index = copies.take()
            self.recv_index = copies.take(3)
            self.mine = self.target == y
            if len(halves) == 2:
                self.gives = self.takes = jnp.bool_(True)
            else:
                self.gives, self.takes = k != halves[0], k == halves[0]
            self.pair = copies.make(
                grams.at[1 - k, e, self.place], pairs.at[e, self.place], sibling, self.pair_index
            )

        def send_pair(self):
            pl.when(self.gives)(lambda: self.pair.start())

        def outgoing(self, panel):
            back = wrap(y - self.target)
            device = {"grid": self.target * 2 + k}
            slot = jnp.maximum(back - 1, 0)
            if panel:
                target = arrived_panel.at[slot, pl.ds(self.start, self.rows)]
            else:
                target = arrived.at[slot, self.place]
            return copies.make(
                grams.at[k, self.e, self.place], target, device, self.send_index, self.recv_index + slot
            )

        def send_on(self):
            @pl.when(self.takes)
            def _():
                self.pair.wait_recv()
                grams[k, self.e, self.place, :] = grams[k, self.e, self.place, :] + pairs[self.e, self.place, :]

                @pl.when(jnp.logical_and(self.is_panel, y == 0))
                def _():
                    rows = pl.ds(self.i * TILE + self.start, self.rows)
                    grams[k, self.e, self.place, :] = grams[k, self.e, self.place, :] + base_ref[rows, :]

                @pl.when(jnp.logical_not(self.mine))
                def _():
                    @pl.when(self.is_panel)
                    def _():
                        self.outgoing(True).start()

                    @pl.when(jnp.logical_not(self.is_panel))
                    def _():
                        self.outgoing(False).start()

        def collect(self):
            @pl.when(jnp.logical_and(self.takes, self.mine))
            def _():
                total = grams.at[k, self.e, self.place]

                @pl.when(self.is_panel)
                def _():
                    rows = pl.ds(self.start, self.rows)
                    for slot in range(3):
                        landed = arrived_panel.at[slot, rows]
                        copies.make(landed, landed, sibling, self.send_index, self.recv_index + slot).wait_recv()
                    panel_ref[2 * c + k, pl.ds(self.i * TILE + self.start, self.rows), :] = (
                        total[...] + arrived_panel[0, rows, :] + arrived_panel[1, rows, :] + arrived_panel[2, rows, :]
                    )

                @pl.when(jnp.logical_not(self.is_panel))
                def _():
                    for slot in range(3):
                        landed = arrived.at[slot, self.place]
                        copies.make(landed, landed, sibling, self.send_index, self.recv_index + slot).wait_recv()
                    rows = pl.ds(self.i * TILE + self.start, self.rows)
                    share_ref[rows, :] = (
                        total[...]
                        + arrived[0, self.place, :]
                        + arrived[1, self.place, :]
                        + arrived[2, self.place, :]
                        + base_ref[rows, :]
                    )

        def finish(self):
            pl.when(self.gives)(lambda: self.pair.wait_send())

            @pl.when(jnp.logical_and(self.takes, jnp.logical_not(self.mine)))
            def _():
                self.outgoing(False).wait_send()

    units = [Unit(d, e, (0, 1)) for e in range(3) for d in range(3)]
    early = list(units)
    for e in range(3):
        product = gram(0, 3 * TILE, column_slots[e])
        grams[0, e, pl.ds(0, 3 * TILE), :] = product[:, :HALF]
        grams[1, e, pl.ds(0, 3 * TILE), :] = product[:, HALF:]
        for unit in early[3 * e : 3 * e + 3]:
            unit.send_pair()
    for unit in early:
        unit.send_on()
    for unit in early:
        unit.collect()

    in_diag = jnp.logical_and(c < 2, y < 2)

    @pl.when(jnp.logical_and(in_diag, r == 0))
    def _():
        diag_ref[y, 2 * c + k, :, :] = panel_ref[2 * c + k, pl.ds(y * TILE, TILE), :]

    diag_z = Spread(copies, step_z, r, in_diag, diag_ref.at[jnp.minimum(y, 1), jnp.minimum(2 * c, 2) + k])
    diag_x = [
        Spread(copies, step_x, wrap(c - t), y < 2, diag_ref.at[jnp.minimum(y, 1), 2 * t + k]) for t in range(2)
    ]
    diag_y = [
        Spread(copies, step_y, wrap(y - i), jnp.bool_(True), diag_ref.at[i, 2 * t + k])
        for i in range(2)
        for t in range(2)
    ]
    diag_z.start()

    def late_stage(half):
        for base_slot in (0, 3):
            for part in (2 * half, 2 * half + 1):
                second_hop[base_slot, part].wait_recv()
        stage = []
        start = half * HALF
        rows = pl.ds(3 * TILE + start, HALF)
        for e in range(3):
            product = gram(3 * TILE + start, HALF, column_slots[e])
            grams[0, e, rows, :] = product[:, :HALF]
            grams[1, e, rows, :] = product[:, HALF:]
            unit = Unit(3, e, (0, 1), start, HALF)
            unit.send_pair()
            stage.append(unit)
        if half == 1:
            grams[0, 3, rows, :] = gram(3 * TILE + start, HALF, 6, 0, HALF)
            unit = Unit(3, 3, (0,), start, HALF)
            unit.send_pair()
            stage.append(unit)
        height = 3 * TILE + start + HALF
        grams[half, 3, pl.ds(0, height), :] = gram(0, height, 6, start, HALF)
        for d in range(4):
            unit = Unit(d, 3, (half,), 0, HALF if d == 3 and half == 0 else TILE)
            unit.send_pair()
            stage.append(unit)
        return stage

    stage = late_stage(0)
    units += stage
    diag_z.forward()
    for unit in stage:
        unit.send_on()
    diag_z.arrive()
    for spread in diag_x:
        spread.start()
    stage = late_stage(1)
    units += stage
    for spread in diag_x:
        spread.forward()
    for unit in stage:
        unit.send_on()
    for unit in units[len(early) :]:
        unit.collect()

    panel_x = [
        Spread(copies, step_x, wrap(c - t), jnp.bool_(True), panel_ref.at[2 * t + k, pl.ds(y * TILE, TILE)])
        for t in range(2)
    ]
    for spread in panel_x:
        spread.start()
    has_share = jnp.logical_not(jnp.logical_and(c < 2, y == 0))

    @pl.when(jnp.logical_and(has_share, r == 0))
    def _():
        mirror_ref[...] = share_ref[pl.ds(0, 2 * TILE), :]

    mirror_z = Spread(copies, step_z, r, has_share, mirror_ref)
    mirror_z.start()
    for spread in diag_x:
        spread.arrive()
    for spread in diag_y:
        spread.start()
    for spread in panel_x:
        spread.forward()
    for spread in panel_x:
        spread.arrive()

    def panel_rows(t, i, start=0, rows=TILE):
        return panel_ref.at[2 * t + k, pl.ds(wrap(i) * TILE + start, rows)]

    around = {}
    for t in range(2):
        for d in (1, -1):
            block = panel_rows(t, y)
            around[t, d] = copies.make(block, block, step_y(d), copies.take())
            around[t, d].start()
    mirror_z.forward()
    for spread in diag_y:
        spread.forward()
    for spread in diag_y:
        spread.arrive()

    handed = []

    def hand(ref):
        copy = copies.make(ref, ref, sibling, copies.take())
        copy.start()
        handed.append(copy)

    for i in range(2):
        for t in range(2):
            hand(diag_ref.at[i, 2 * t + k])
    for t in range(2):
        hand(panel_rows(t, y))
    again = {}
    for t in range(2):
        for d, start in ((1, 0), (-1, HALF)):
            around[t, d].wait_recv()
            block = panel_rows(t, y - d, start, HALF)
            again[t, d] = copies.make(block, block, step_y(d), copies.take())
            again[t, d].start()
            hand(panel_rows(t, y - d))
    for t in range(2):
        again[t, 1].wait_recv()
        again[t, -1].wait_recv()
        hand(panel_rows(t, y + 2))
    mirror_z.arrive()
    for copy in handed:
        copy.wait_recv()

    @pl.when(jnp.logical_not(has_share))
    def _():
        block = 2 * jnp.minimum(c, 1) + k
        share_ref[...] = panel_ref[block]
        for i in range(2):
            mirror_ref[pl.ds(i * TILE, TILE), :] = diag_ref[i, block]

    for copy in [*first_hop.values(), *second_hop.values(), *around.values(), *again.values(), *handed]:
        copy.wait_send()
    for unit in units:
        unit.finish()
    for spread in [diag_z, *diag_x, *diag_y, *panel_x, mirror_z]:
        spread.finish()


def dot(a, b, contract=(1, 0), precision=HIGHEST):
    return lax.dot_general(
        a, b, (((contract[0],), (contract[1],)), ((), ())),
        precision=precision, preferred_element_type=jnp.float32,
    )


def row_sum_bound(matrix):
    return jnp.max(jnp.sum(jnp.abs(matrix), axis=1, keepdims=True))


def inverse(matrix, x_ref, e_ref):
    size = matrix.shape[0]
    same = lax.broadcasted_iota(jnp.int32, (size, size), 0) == lax.broadcasted_iota(jnp.int32, (size, size), 1)
    identity = jnp.where(same, 1.0, 0.0).astype(jnp.float32)
    diagonal = jnp.where(same, matrix, 0.0)
    across = lax.rsqrt(jnp.sum(diagonal, axis=0, keepdims=True))
    down = lax.rsqrt(jnp.sum(diagonal, axis=1, keepdims=True))
    scaled = matrix * across * down
    start = identity * (2.0 / (1.0 + row_sum_bound(scaled)))

    def coarse(_, x):
        coarse_x = x.astype(jnp.bfloat16)
        gap = identity - dot(scaled.astype(jnp.bfloat16), coarse_x, precision=None)
        return x + dot(coarse_x, gap.astype(jnp.bfloat16), precision=None)

    x_ref[...] = lax.fori_loop(0, 4, coarse, start)
    gap = identity - dot(scaled, x_ref[...])
    e_ref[...] = gap
    bound = row_sum_bound(gap)

    @pl.when(jnp.logical_not(bound < 0.5))
    def _():
        x_ref[...] = start
        e_ref[...] = identity - dot(scaled, start)

    def more(state):
        count, bound, last = state
        return jnp.logical_and(count < 60, jnp.logical_and(bound > 1e-5, jnp.logical_or(bound > 0.5, bound < last)))

    def step(state):
        count, bound, last = state
        x_ref[...] = x_ref[...] + dot(x_ref[...], e_ref[...])
        gap = identity - dot(scaled, x_ref[...])
        e_ref[...] = gap
        return count + 1, row_sum_bound(gap), bound

    bound = row_sum_bound(e_ref[...])
    lax.while_loop(more, step, (jnp.int32(0), bound, jnp.float32(jnp.inf)))
    x_ref[...] = x_ref[...] + dot(x_ref[...], e_ref[...])
    x_ref[...] = x_ref[...] * across * down


def eliminate_kernel(share_ref, panel_ref, diag_ref, mirror_ref, schur_ref, lower_ref, x_ref, gap_ref):
    def block(i, t):
        return jnp.concatenate([diag_ref[i, 2 * t], diag_ref[i, 2 * t + 1]], axis=1)

    cross = block(1, 0)
    inverse(block(0, 0), x_ref, gap_ref)
    first = x_ref[...]
    ratio = dot(cross, first)
    inverse(block(1, 1) - dot(ratio, cross, (1, 1)), x_ref, gap_ref)
    second = x_ref[...]
    left = jnp.concatenate([panel_ref[0], panel_ref[1]], axis=1)
    right = jnp.concatenate([panel_ref[2], panel_ref[3]], axis=1)
    lower_first = dot(left, first)
    lower_ref[:, :TILE] = lower_first
    lower_second = dot(right - dot(left, ratio, (1, 1)), second)
    lower_ref[:, TILE:] = lower_second
    above = mirror_ref[:TILE, :]
    below = mirror_ref[TILE:, :] - dot(ratio, above)
    schur_ref[...] = share_ref[...] - dot(lower_first, above) - dot(lower_second, below)


def shards(updates, row_mask, base):
    vmem = pl.BlockSpec(memory_space=pltpu.VMEM)
    smem = pl.BlockSpec(memory_space=pltpu.SMEM)
    f32 = jnp.float32
    semaphores = 320
    share, panel, diag, mirror = pl.pallas_call(
        gather_kernel,
        out_shape=(
            jax.ShapeDtypeStruct((ROWS, HALF), f32),
            jax.ShapeDtypeStruct((4, ROWS, HALF), f32),
            jax.ShapeDtypeStruct((2, 4, TILE, HALF), f32),
            jax.ShapeDtypeStruct((2 * TILE, HALF), f32),
        ),
        in_specs=[vmem, smem, vmem],
        out_specs=(vmem,) * 4,
        scratch_shapes=[
            pltpu.VMEM((7 * TILE, DEPTH), jnp.bfloat16),
            pltpu.VMEM((2, 4, ROWS, HALF), f32),
            pltpu.VMEM((4, ROWS, HALF), f32),
            pltpu.VMEM((3, ROWS, HALF), f32),
            pltpu.VMEM((3, TILE, HALF), f32),
            pltpu.SemaphoreType.DMA((semaphores,)),
            pltpu.SemaphoreType.DMA((semaphores,)),
        ],
        compiler_params=pltpu.CompilerParams(
            collective_id=0, has_side_effects=True, vmem_limit_bytes=56 << 20
        ),
        cost_estimate=pl.CostEstimate(flops=8 << 30, bytes_accessed=8 << 20, transcendentals=0),
    )(updates[0], row_mask, base[:, 0, :])
    schur, lower = pl.pallas_call(
        eliminate_kernel,
        out_shape=(jax.ShapeDtypeStruct((ROWS, HALF), f32), jax.ShapeDtypeStruct((ROWS, 2 * TILE), f32)),
        in_specs=[vmem] * 4,
        out_specs=(vmem,) * 2,
        scratch_shapes=[pltpu.VMEM((TILE, TILE), f32)] * 2,
        compiler_params=pltpu.CompilerParams(vmem_limit_bytes=48 << 20),
        cost_estimate=pl.CostEstimate(flops=1 << 30, bytes_accessed=8 << 20, transcendentals=0),
    )(share, panel, diag, mirror)
    return schur[:, None, :], lower


def solution(mesh):
    placed = (P("grid", ("prow", "pcol"), None), P("grid", None), P("prow", "pcol", "grid"))
    return jax.shard_map(
        shards,
        mesh=mesh,
        in_specs=placed,
        out_specs=(P("prow", "pcol", "grid"), P("prow", None)),
        check_vma=False,
    )
```

```python
import jax
import jax.numpy as jnp
from jax import lax
from jax.experimental import pallas as pl
from jax.experimental.pallas import tpu as pltpu
from jax.sharding import PartitionSpec as P

TILE = 256
HALF = 128
DEPTH = 4096
ROWS = 1024
CHUNK = 64
SENDS = 146
RECEIVES = 206
MESH = pl.DeviceIdType.MESH
HIGHEST = lax.Precision.HIGHEST
OFFSETS = (0, 1, 3, 2)


def wrap(value):
    return lax.rem(value + 4, 4)


class Copies:
    def __init__(self, send_sems, recv_sems):
        self.send_sems, self.recv_sems, self.sends, self.receives = send_sems, recv_sems, 0, 0

    def take(self, sends=1, receives=1):
        first = self.sends, self.receives
        self.sends, self.receives = self.sends + sends, self.receives + receives
        return first

    def make(self, src, dst, device, index):
        return pltpu.make_async_remote_copy(
            src_ref=src,
            dst_ref=dst,
            send_sem=self.send_sems.at[index[0]],
            recv_sem=self.recv_sems.at[index[1]],
            device_id=device,
            device_id_type=MESH,
        )


class Spread:
    def __init__(self, copies, step, place, holds, block):
        rows = block.shape[0] // 2
        self.place, self.holds = place, holds
        send, receive = copies.take(2, 2)
        upper, lower = block.at[pl.ds(0, rows)], block.at[pl.ds(rows, rows)]
        self.up = copies.make(block, block, step(1), (send, receive))
        self.down = copies.make(block, block, step(-1), (send + 1, receive + 1))
        self.up_half = copies.make(upper, upper, step(1), (send, receive))
        self.down_half = copies.make(lower, lower, step(-1), (send + 1, receive + 1))

    def when(self, place):
        return pl.when(jnp.logical_and(self.holds, self.place == place))

    def start(self):
        @pl.when(jnp.logical_and(self.holds, self.place == 0))
        def _():
            self.up.start()
            self.down.start()

    def forward(self):
        @self.when(1)
        def _():
            self.up.wait_recv()
            self.up_half.start()

        @self.when(3)
        def _():
            self.down.wait_recv()
            self.down_half.start()

    def arrive(self):
        @self.when(2)
        def _():
            self.up_half.wait_recv()
            self.down_half.wait_recv()

    def finish(self):
        @self.when(0)
        def _():
            self.up.wait_send()
            self.down.wait_send()

        @self.when(1)
        def _():
            self.up_half.wait_send()

        @self.when(3)
        def _():
            self.down_half.wait_send()


def gather_kernel(
    u_ref, mask_ref, base_ref, share_ref, panel_ref, diag_ref, mirror_ref,
    tiles, grams, pairs, relays, arrived, arrived_panel, send_sems, recv_sems,
):
    grid = lax.axis_index("grid")
    r = lax.axis_index("prow")
    c = lax.axis_index("pcol")
    y, k = grid // 2, lax.rem(grid, 2)
    copies = Copies(send_sems, recv_sems)
    sibling = {"grid": y * 2 + 1 - k}

    def step_x(d):
        return {"pcol": wrap(c + d)}

    def step_y(d):
        return {"grid": wrap(y + d) * 2 + k}

    def step_z(d):
        return {"prow": wrap(r + d)}

    barrier = pltpu.get_barrier_semaphore()
    others = [step_x(1), step_x(-1), step_z(1), step_z(-1), step_y(1), step_y(-1), sibling]
    for other in others:
        pl.semaphore_signal(barrier, inc=1, device_id=other, device_id_type=MESH)
    pl.semaphore_wait(barrier, len(others))

    keep = mask_ref[0, r * 4 + c] > 0
    first_hop, second_hop = {}, {}
    streams = [(step, d, base_slot) for step, base_slot in ((step_x, 0), (step_z, 3)) for d in (-1, 1)]

    def rows_of(slot, start, size):
        return tiles.at[pl.ds(slot * TILE + start, size)]

    for part in range(TILE // CHUNK):
        start = part * CHUNK
        value = u_ref[pl.ds(start, CHUNK), :]
        tiles[pl.ds(start, CHUNK), :] = jnp.where(keep, value, jnp.zeros_like(value))
        for step, d, base_slot in streams:
            slot = base_slot + (1 if d == -1 else 2)
            copy = copies.make(rows_of(0, start, CHUNK), rows_of(slot, start, CHUNK), step(d), copies.take())
            copy.start()
            first_hop[base_slot, d, part] = copy

    def gram(rows_start, rows, slot, columns_start=0, columns=TILE):
        return lax.dot_general(
            tiles[pl.ds(rows_start, rows), :],
            tiles[pl.ds(slot * TILE + columns_start, columns), :],
            (((1,), (1,)), ((), ())),
            preferred_element_type=jnp.float32,
        )

    column_slots = (0, 4, 5, 6)

    def gram_into(d, start, rows, e):
        product = gram(d * TILE + start, rows, column_slots[e])
        place = pl.ds(d * TILE + start, rows)
        grams[0, e, place, :] = product[:, :HALF]
        grams[1, e, place, :] = product[:, HALF:]

    class Unit:
        def __init__(self, d, e, halves, start=0, rows=TILE, panel=None):
            self.d, self.e, self.halves, self.start, self.rows, self.panel = d, e, halves, start, rows, panel
            self.place = pl.ds(d * TILE + start, rows)
            cut = rows // 2
            self.parts = [pl.ds(d * TILE + start + n * cut, cut) for n in range(2)]
            self.panel_parts = [pl.ds(start + n * cut, cut) for n in range(2)]
            self.q = wrap(r + OFFSETS[e])
            self.i = wrap(c + OFFSETS[d])
            self.is_panel = jnp.logical_and(c < 2, self.q == 0)
            self.target = jnp.where(self.is_panel, self.i, self.q)
            self.back = wrap(y - self.target)
            self.pair_index = copies.take(0, 0) if panel else copies.take()
            self.send_index, self.recv_index = copies.take(2, 4)
            if len(halves) == 2:
                self.gives = self.takes = jnp.bool_(True)
            else:
                self.gives, self.takes = k != halves[0], k == halves[0]
            if not panel:
                self.pair = copies.make(
                    grams.at[1 - k, e, self.place], pairs.at[e, self.place], sibling, self.pair_index
                )
            self.holds = self.takes
            if panel is not None:
                self.holds = jnp.logical_and(self.takes, self.is_panel if panel else jnp.logical_not(self.is_panel))

        def send_pair(self):
            pl.when(self.gives)(lambda: self.pair.start())

        def when(self, back):
            return pl.when(jnp.logical_and(self.holds, self.back == back))

        def relay(self, part):
            return copies.make(
                grams.at[k, self.e, self.parts[part]], relays.at[self.e, self.parts[part]],
                step_y(2 * part - 1), (self.send_index + part, self.recv_index),
            )

        def last(self, side, part, panel):
            if panel:
                landing = arrived_panel.at[side, self.panel_parts[part]]
            else:
                landing = arrived.at[side, self.parts[part]]
            return copies.make(
                grams.at[k, self.e, self.parts[part]], landing, step_y(2 * side - 1),
                (self.send_index + part, self.recv_index + 2 * side + part),
            )

        def send_last(self, side, part):
            if self.panel is not None:
                self.last(side, part, self.panel).start()
                return

            @pl.when(self.is_panel)
            def _():
                self.last(side, part, True).start()

            @pl.when(jnp.logical_not(self.is_panel))
            def _():
                self.last(side, part, False).start()

        def send_on(self):
            if not self.panel:

                @pl.when(self.takes)
                def _():
                    self.pair.wait_recv()
                    grams[k, self.e, self.place, :] = grams[k, self.e, self.place, :] + pairs[self.e, self.place, :]

            if self.panel is not False:

                @pl.when(jnp.logical_and(self.holds, jnp.logical_and(self.is_panel, y == 0)))
                def _():
                    rows = pl.ds(self.i * TILE + self.start, self.rows)
                    grams[k, self.e, self.place, :] = grams[k, self.e, self.place, :] + base_ref[rows, :]

            @self.when(2)
            def _():
                self.relay(0).start()
                self.relay(1).start()

            for side in range(2):

                @self.when(1 + 2 * side)
                def _():
                    self.send_last(side, 1 - side)

        def relay_on(self):
            for side in range(2):

                @self.when(1 + 2 * side)
                def _():
                    part = self.parts[side]
                    self.relay(side).wait_recv()
                    grams[k, self.e, part, :] = grams[k, self.e, part, :] + relays[self.e, part, :]
                    self.send_last(side, side)

        def collect(self):
            @self.when(0)
            def _():
                for side in range(2):
                    for part in (1 - side, side):
                        self.last(side, part, bool(self.panel)).wait_recv()
                if self.panel is None:
                    pl.when(self.is_panel)(lambda: self.add_panel())
                    pl.when(jnp.logical_not(self.is_panel))(lambda: self.add_share())
                elif self.panel:
                    self.add_panel()
                else:
                    self.add_share()

        def add_panel(self):
            rows = pl.ds(self.i * TILE + self.start, self.rows)
            landed = pl.ds(self.start, self.rows)
            panel_ref[2 * c + k, rows, :] = (
                grams[k, self.e, self.place, :] + arrived_panel[0, landed, :] + arrived_panel[1, landed, :]
            )

        def add_share(self):
            done = 0
            while done < self.rows:
                d, start = (self.d * TILE + self.start + done) // TILE, (self.start + done) % TILE
                number = min(self.rows - done, TILE - start)
                rows = pl.ds(wrap(c + OFFSETS[d]) * TILE + start, number)
                place = pl.ds(d * TILE + start, number)
                share_ref[rows, :] = (
                    grams[k, self.e, place, :] + arrived[0, place, :] + arrived[1, place, :] + base_ref[rows, :]
                )
                done += number

        def finish(self):
            if not self.panel:
                pl.when(self.gives)(lambda: self.pair.wait_send())

            @self.when(2)
            def _():
                self.relay(0).wait_send()
                self.relay(1).wait_send()

            for side in range(2):

                @self.when(1 + 2 * side)
                def _():
                    self.last(side, 0, bool(self.panel)).wait_send()
                    self.last(side, 1, bool(self.panel)).wait_send()

    def each(items, name):
        for item in items:
            getattr(item, name)()

    gram_into(0, 0, TILE, 0)
    opening = [Unit(0, 0, (0, 1))]
    each(opening, "send_pair")
    for part in range(TILE // CHUNK):
        start = part * CHUNK
        for step, d, base_slot in streams:
            first_hop[base_slot, d, part].wait_recv()
            if part % 2 == (0 if d == 1 else 1):
                slot = base_slot + (1 if d == -1 else 2)
                copy = copies.make(
                    rows_of(slot, start, CHUNK), rows_of(base_slot + 3, start, CHUNK), step(d), copies.take()
                )
                copy.start()
                second_hop[base_slot, part] = copy
        if part == 0:
            each(opening, "send_on")
        if part == 1:
            halves = []
            for d in (1, 2):
                gram_into(d, 0, HALF, 0)
                halves.append(Unit(d, 0, (0, 1), 0, HALF))
                halves[-1].send_pair()
            for e in (1, 2):
                grams[0, e, pl.ds(0, TILE), :] = gram(0, TILE, column_slots[e], 0, HALF)
                halves.append(Unit(0, e, (0,)))
                halves[-1].send_pair()
            each(opening, "relay_on")
            each(halves, "send_on")
        if part == 2:
            each(halves, "relay_on")

    in_diag = jnp.logical_and(c < 2, y < 2)

    diag_z = Spread(copies, step_z, r, in_diag, diag_ref.at[jnp.minimum(y, 1), jnp.minimum(2 * c, 2) + k])
    diag_x = [
        Spread(copies, step_x, wrap(c - t), y < 2, diag_ref.at[jnp.minimum(y, 1), 2 * t + k]) for t in range(2)
    ]
    diag_y = [
        Spread(copies, step_y, wrap(y - i), jnp.bool_(True), diag_ref.at[i, 2 * t + k])
        for i in range(2)
        for t in range(2)
    ]
    def late_stage(half):
        for base_slot in (0, 3):
            for part in (2 * half, 2 * half + 1):
                second_hop[base_slot, part].wait_recv()
        stage = []
        start = half * HALF
        rows = pl.ds(3 * TILE + start, HALF)
        height = 3 * TILE + start + HALF
        grams[half, 3, pl.ds(0, height), :] = gram(0, height, 6, start, HALF)
        stage.append(Unit(0, 3, (half,), 0, height, panel=False))
        stage[-1].send_pair()
        for d in range(4):
            stage.append(Unit(d, 3, (half,), 0, HALF if d == 3 and half == 0 else TILE, panel=True))
        if half == 1:
            grams[0, 3, rows, :] = gram(3 * TILE + start, HALF, 6, 0, HALF)
            stage.append(Unit(3, 3, (0,), start, HALF))
            stage[-1].send_pair()
        for e in range(3):
            product = gram(3 * TILE + start, HALF, column_slots[e])
            grams[0, e, rows, :] = product[:, :HALF]
            grams[1, e, rows, :] = product[:, HALF:]
            unit = Unit(3, e, (0, 1), start, HALF)
            unit.send_pair()
            stage.append(unit)
        return stage

    rest = [[], [], []]
    for d in (1, 2):
        gram_into(d, HALF, HALF, 0)
        rest[0].append(Unit(d, 0, (0, 1), HALF, HALF))
        rest[0][-1].send_pair()
    for e in (1, 2):
        grams[1, e, pl.ds(0, TILE), :] = gram(0, TILE, column_slots[e], HALF, HALF)
        product = gram(TILE, 2 * TILE, column_slots[e])
        grams[0, e, pl.ds(TILE, 2 * TILE), :] = product[:, :HALF]
        grams[1, e, pl.ds(TILE, 2 * TILE), :] = product[:, HALF:]
        rest[e] = [Unit(0, e, (1,)), Unit(1, e, (0, 1)), Unit(2, e, (0, 1))]
        each(rest[e], "send_pair")
        each(rest[e - 1], "send_on")
        if e == 2:
            each(rest[0], "relay_on")
    each(rest[2], "send_on")
    each([*opening, *halves, *rest[0]], "collect")

    @pl.when(jnp.logical_and(in_diag, r == 0))
    def _():
        diag_ref[y, 2 * c + k, :, :] = panel_ref[2 * c + k, pl.ds(y * TILE, TILE), :]

    diag_z.start()
    each(rest[1], "relay_on")
    first_late = late_stage(0)
    each(first_late, "send_on")
    each(rest[2], "relay_on")
    each(first_late, "relay_on")
    second_late = late_stage(1)
    each(second_late, "send_on")
    each([*rest[1], *rest[2]], "collect")
    diag_z.forward()
    each(second_late, "relay_on")
    each(first_late, "collect")
    diag_z.arrive()
    each(diag_x, "start")
    each(second_late, "collect")

    handed = []

    def hand(ref):
        copy = copies.make(ref, ref, sibling, copies.take())
        copy.start()
        handed.append(copy)

    def panel_rows(t, i, start=0, rows=TILE):
        return panel_ref.at[2 * t + k, pl.ds(wrap(i) * TILE + start, rows)]

    panel_x = [
        Spread(copies, step_x, wrap(c - t), jnp.bool_(True), panel_ref.at[2 * t + k, pl.ds(y * TILE, TILE)])
        for t in range(2)
    ]
    each(panel_x, "start")
    has_share = jnp.logical_not(jnp.logical_and(c < 2, y == 0))

    @pl.when(jnp.logical_and(has_share, r == 0))
    def _():
        mirror_ref[...] = share_ref[pl.ds(0, 2 * TILE), :]

    mirror_z = Spread(copies, step_z, r, has_share, mirror_ref)
    mirror_z.start()
    each(diag_x, "forward")
    each(panel_x, "forward")
    each(diag_x, "arrive")
    each(diag_y, "start")
    each(panel_x, "arrive")
    around, again = {}, {}
    for t in range(2):
        for d in (1, -1):
            block = panel_rows(t, y)
            around[t, d] = copies.make(block, block, step_y(d), copies.take())
            around[t, d].start()
        hand(panel_rows(t, y))
    mirror_z.forward()
    each(diag_y, "forward")
    for t in range(2):
        for d, start in ((1, 0), (-1, HALF)):
            around[t, d].wait_recv()
            block = panel_rows(t, y - d, start, HALF)
            again[t, d] = copies.make(block, block, step_y(d), copies.take())
            again[t, d].start()
            hand(panel_rows(t, y - d))
    each(diag_y, "arrive")
    for i in range(2):
        for t in range(2):
            hand(diag_ref.at[i, 2 * t + k])
    for t in range(2):
        again[t, 1].wait_recv()
        again[t, -1].wait_recv()
        hand(panel_rows(t, y + 2))
    mirror_z.arrive()
    each(handed, "wait_recv")

    @pl.when(jnp.logical_not(has_share))
    def _():
        block = 2 * jnp.minimum(c, 1) + k
        share_ref[...] = panel_ref[block]
        for i in range(2):
            mirror_ref[pl.ds(i * TILE, TILE), :] = diag_ref[i, block]

    for copy in [*first_hop.values(), *second_hop.values(), *around.values(), *again.values(), *handed]:
        copy.wait_send()
    for unit in [*opening, *halves, *rest[0], *rest[1], *rest[2], *first_late, *second_late]:
        unit.finish()
    for spread in [diag_z, *diag_x, *diag_y, *panel_x, mirror_z]:
        spread.finish()


def dot(a, b, contract=(1, 0), precision=HIGHEST):
    return lax.dot_general(
        a, b, (((contract[0],), (contract[1],)), ((), ())),
        precision=precision, preferred_element_type=jnp.float32,
    )


def row_sum_bound(matrix):
    return jnp.max(jnp.sum(jnp.abs(matrix), axis=1, keepdims=True))


def inverse(matrix, x_ref, e_ref):
    size = matrix.shape[0]
    same = lax.broadcasted_iota(jnp.int32, (size, size), 0) == lax.broadcasted_iota(jnp.int32, (size, size), 1)
    identity = jnp.where(same, 1.0, 0.0).astype(jnp.float32)
    diagonal = jnp.where(same, matrix, 0.0)
    across = lax.rsqrt(jnp.sum(diagonal, axis=0, keepdims=True))
    down = lax.rsqrt(jnp.sum(diagonal, axis=1, keepdims=True))
    scaled = matrix * across * down
    start = identity * (2.0 / (1.0 + row_sum_bound(scaled)))

    def coarse(_, x):
        coarse_x = x.astype(jnp.bfloat16)
        gap = identity - dot(scaled.astype(jnp.bfloat16), coarse_x, precision=None)
        return x + dot(coarse_x, gap.astype(jnp.bfloat16), precision=None)

    x_ref[...] = lax.fori_loop(0, 4, coarse, start)
    gap = identity - dot(scaled, x_ref[...])
    e_ref[...] = gap
    bound = row_sum_bound(gap)

    @pl.when(jnp.logical_not(bound < 0.5))
    def _():
        x_ref[...] = start
        e_ref[...] = identity - dot(scaled, start)

    def more(state):
        count, bound, last = state
        return jnp.logical_and(count < 60, jnp.logical_and(bound > 1e-3, jnp.logical_or(bound > 0.5, bound < last)))

    def step(state):
        count, bound, last = state
        x_ref[...] = x_ref[...] + dot(x_ref[...], e_ref[...])
        gap = identity - dot(scaled, x_ref[...])
        e_ref[...] = gap
        return count + 1, row_sum_bound(gap), bound

    bound = row_sum_bound(e_ref[...])
    lax.while_loop(more, step, (jnp.int32(0), bound, jnp.float32(jnp.inf)))
    x_ref[...] = x_ref[...] + dot(x_ref[...], e_ref[...])
    x_ref[...] = x_ref[...] * across * down


def eliminate_kernel(
    share_in, panel_in, diag_in, mirror_in, schur_out, lower_out,
    share_ref, panel_ref, diag_ref, mirror_ref, schur_ref, lower_ref, x_ref, gap_ref, in_sems, out_sems,
):
    pairs = ((diag_in, diag_ref), (mirror_in, mirror_ref), (panel_in, panel_ref), (share_in, share_ref))
    loads = [pltpu.make_async_copy(src, dst, in_sems.at[n]) for n, (src, dst) in enumerate(pairs)]
    for load in loads:
        load.start()

    def block(i, t):
        return jnp.concatenate([diag_ref[i, 2 * t], diag_ref[i, 2 * t + 1]], axis=1)

    loads[0].wait()
    cross = block(1, 0)
    inverse(block(0, 0), x_ref, gap_ref)
    first = x_ref[...]
    ratio = dot(cross, first)
    inverse(block(1, 1) - dot(ratio, cross, (1, 1)), x_ref, gap_ref)
    second = x_ref[...]
    for load in loads[1:]:
        load.wait()
    above = mirror_ref[:TILE, :]
    below = mirror_ref[TILE:, :] - dot(ratio, above)
    stores = []
    for i in range(4):
        rows = pl.ds(i * TILE, TILE)
        left = jnp.concatenate([panel_ref[0, rows, :], panel_ref[1, rows, :]], axis=1)
        right = jnp.concatenate([panel_ref[2, rows, :], panel_ref[3, rows, :]], axis=1)
        lower_first = dot(left, first)
        lower_second = dot(right - dot(left, ratio, (1, 1)), second)
        lower_ref[rows, :TILE] = lower_first
        lower_ref[rows, TILE:] = lower_second
        schur_ref[rows, :] = share_ref[rows, :] - dot(lower_first, above) - dot(lower_second, below)
        for n, (src, dst) in enumerate(((lower_ref, lower_out), (schur_ref, schur_out))):
            store = pltpu.make_async_copy(src.at[rows], dst.at[rows], out_sems.at[2 * i + n])
            store.start()
            stores.append(store)
    for store in stores:
        store.wait()


def shards(updates, row_mask, base):
    vmem = pl.BlockSpec(memory_space=pltpu.VMEM)
    smem = pl.BlockSpec(memory_space=pltpu.SMEM)
    f32 = jnp.float32
    staged = (
        jax.ShapeDtypeStruct((ROWS, HALF), f32),
        jax.ShapeDtypeStruct((4, ROWS, HALF), f32),
        jax.ShapeDtypeStruct((2, 4, TILE, HALF), f32),
        jax.ShapeDtypeStruct((2 * TILE, HALF), f32),
    )
    between = pl.pallas_call(
        gather_kernel,
        out_shape=staged,
        in_specs=[vmem, smem, vmem],
        out_specs=(vmem,) * 4,
        scratch_shapes=[
            pltpu.VMEM((7 * TILE, DEPTH), jnp.bfloat16),
            pltpu.VMEM((2, 4, ROWS, HALF), f32),
            pltpu.VMEM((4, ROWS, HALF), f32),
            pltpu.VMEM((4, ROWS, HALF), f32),
            pltpu.VMEM((2, ROWS, HALF), f32),
            pltpu.VMEM((2, TILE, HALF), f32),
            pltpu.SemaphoreType.DMA((SENDS,)),
            pltpu.SemaphoreType.DMA((RECEIVES,)),
        ],
        compiler_params=pltpu.CompilerParams(
            collective_id=0, has_side_effects=True, vmem_limit_bytes=56 << 20
        ),
        cost_estimate=pl.CostEstimate(flops=8 << 30, bytes_accessed=8 << 20, transcendentals=0),
    )(updates[0], row_mask, base[:, 0, :])
    result = (jax.ShapeDtypeStruct((ROWS, HALF), f32), jax.ShapeDtypeStruct((ROWS, 2 * TILE), f32))
    anywhere = pl.BlockSpec(memory_space=pl.ANY)
    schur, lower = pl.pallas_call(
        eliminate_kernel,
        out_shape=result,
        in_specs=[anywhere] * 4,
        out_specs=(anywhere,) * 2,
        scratch_shapes=[
            *[pltpu.VMEM(array.shape, f32) for array in (*staged, *result)],
            *[pltpu.VMEM((TILE, TILE), f32)] * 2,
            pltpu.SemaphoreType.DMA((4,)),
            pltpu.SemaphoreType.DMA((8,)),
        ],
        compiler_params=pltpu.CompilerParams(vmem_limit_bytes=60 << 20),
        cost_estimate=pl.CostEstimate(flops=1 << 30, bytes_accessed=8 << 20, transcendentals=0),
    )(*between)
    return schur[:, None, :], lower


def solution(mesh):
    placed = (P("grid", ("prow", "pcol"), None), P("grid", None), P("prow", "pcol", "grid"))
    return jax.shard_map(
        shards,
        mesh=mesh,
        in_specs=placed,
        out_specs=(P("prow", "pcol", "grid"), P("prow", None)),
        check_vma=False,
    )
```

```python
import jax
import jax.numpy as jnp
from jax import lax
from jax.experimental import pallas as pl
from jax.experimental.pallas import tpu as pltpu
from jax.sharding import PartitionSpec as P

TILE = 256
HALF = 128
DEPTH = 4096
ROWS = 1024
CHUNK = 64
SENDS = 145
RECEIVES = 205
MESH = pl.DeviceIdType.MESH
HIGHEST = lax.Precision.HIGHEST
OFFSETS = (0, 1, 3, 2)


def wrap(value):
    return lax.rem(value + 4, 4)


class Copies:
    def __init__(self, send_sems, recv_sems):
        self.send_sems, self.recv_sems, self.sends, self.receives = send_sems, recv_sems, 0, 0

    def take(self, sends=1, receives=1):
        first = self.sends, self.receives
        self.sends, self.receives = self.sends + sends, self.receives + receives
        return first

    def make(self, src, dst, device, index):
        return pltpu.make_async_remote_copy(
            src_ref=src,
            dst_ref=dst,
            send_sem=self.send_sems.at[index[0]],
            recv_sem=self.recv_sems.at[index[1]],
            device_id=device,
            device_id_type=MESH,
        )


class Spread:
    def __init__(self, copies, step, place, holds, block):
        rows = block.shape[0] // 2
        self.place, self.holds = place, holds
        send, receive = copies.take(2, 2)
        upper, lower = block.at[pl.ds(0, rows)], block.at[pl.ds(rows, rows)]
        self.up = copies.make(block, block, step(1), (send, receive))
        self.down = copies.make(block, block, step(-1), (send + 1, receive + 1))
        self.up_half = copies.make(upper, upper, step(1), (send, receive))
        self.down_half = copies.make(lower, lower, step(-1), (send + 1, receive + 1))

    def when(self, place):
        return pl.when(jnp.logical_and(self.holds, self.place == place))

    def start(self):
        @pl.when(jnp.logical_and(self.holds, self.place == 0))
        def _():
            self.up.start()
            self.down.start()

    def forward(self):
        @self.when(1)
        def _():
            self.up.wait_recv()
            self.up_half.start()

        @self.when(3)
        def _():
            self.down.wait_recv()
            self.down_half.start()

    def arrive(self):
        @self.when(2)
        def _():
            self.up_half.wait_recv()
            self.down_half.wait_recv()

    def finish(self):
        @self.when(0)
        def _():
            self.up.wait_send()
            self.down.wait_send()

        @self.when(1)
        def _():
            self.up_half.wait_send()

        @self.when(3)
        def _():
            self.down_half.wait_send()


def gather_kernel(
    u_ref, mask_ref, base_ref, share_ref, panel_ref, diag_ref, mirror_ref,
    tiles, grams, pairs, relays, arrived, arrived_panel, send_sems, recv_sems,
):
    grid = lax.axis_index("grid")
    r = lax.axis_index("prow")
    c = lax.axis_index("pcol")
    y, k = grid // 2, lax.rem(grid, 2)
    copies = Copies(send_sems, recv_sems)
    sibling = {"grid": y * 2 + 1 - k}

    def step_x(d):
        return {"pcol": wrap(c + d)}

    def step_y(d):
        return {"grid": wrap(y + d) * 2 + k}

    def step_z(d):
        return {"prow": wrap(r + d)}

    barrier = pltpu.get_barrier_semaphore()
    others = [step_x(1), step_x(-1), step_z(1), step_z(-1), step_y(1), step_y(-1), sibling]
    for other in others:
        pl.semaphore_signal(barrier, inc=1, device_id=other, device_id_type=MESH)
    pl.semaphore_wait(barrier, len(others))

    keep = mask_ref[0, r * 4 + c] > 0
    first_hop, second_hop = {}, {}
    streams = [(step, d, base_slot) for step, base_slot in ((step_x, 0), (step_z, 3)) for d in (-1, 1)]

    def rows_of(slot, start, size):
        return tiles.at[pl.ds(slot * TILE + start, size)]

    for part in range(TILE // CHUNK):
        start = part * CHUNK
        value = u_ref[pl.ds(start, CHUNK), :]
        tiles[pl.ds(start, CHUNK), :] = jnp.where(keep, value, jnp.zeros_like(value))
        for step, d, base_slot in streams:
            slot = base_slot + (1 if d == -1 else 2)
            copy = copies.make(rows_of(0, start, CHUNK), rows_of(slot, start, CHUNK), step(d), copies.take())
            copy.start()
            first_hop[base_slot, d, part] = copy

    def gram(rows_start, rows, slot, columns_start=0, columns=TILE):
        return lax.dot_general(
            tiles[pl.ds(rows_start, rows), :],
            tiles[pl.ds(slot * TILE + columns_start, columns), :],
            (((1,), (1,)), ((), ())),
            preferred_element_type=jnp.float32,
        )

    column_slots = (0, 4, 5, 6)

    def gram_into(d, start, rows, e):
        product = gram(d * TILE + start, rows, column_slots[e])
        place = pl.ds(d * TILE + start, rows)
        grams[0, e, place, :] = product[:, :HALF]
        grams[1, e, place, :] = product[:, HALF:]

    class Unit:
        def __init__(self, d, e, halves, start=0, rows=TILE, panel=None):
            self.d, self.e, self.halves, self.start, self.rows, self.panel = d, e, halves, start, rows, panel
            self.place = pl.ds(d * TILE + start, rows)
            cut = rows // 2
            self.parts = [pl.ds(d * TILE + start + n * cut, cut) for n in range(2)]
            self.panel_parts = [pl.ds(start + n * cut, cut) for n in range(2)]
            self.q = wrap(r + OFFSETS[e])
            self.i = wrap(c + OFFSETS[d])
            self.is_panel = jnp.logical_and(c < 2, self.q == 0)
            self.target = jnp.where(self.is_panel, self.i, self.q)
            self.back = wrap(y - self.target)
            self.pair_index = copies.take(0, 0) if panel else copies.take()
            self.send_index, self.recv_index = copies.take(2, 4)
            if len(halves) == 2:
                self.gives = self.takes = jnp.bool_(True)
            else:
                self.gives, self.takes = k != halves[0], k == halves[0]
            if not panel:
                self.pair = copies.make(
                    grams.at[1 - k, e, self.place], pairs.at[e, self.place], sibling, self.pair_index
                )
            self.holds = self.takes
            if panel is not None:
                self.holds = jnp.logical_and(self.takes, self.is_panel if panel else jnp.logical_not(self.is_panel))

        def send_pair(self):
            pl.when(self.gives)(lambda: self.pair.start())

        def when(self, back):
            return pl.when(jnp.logical_and(self.holds, self.back == back))

        def relay(self, part):
            return copies.make(
                grams.at[k, self.e, self.parts[part]], relays.at[self.e, self.parts[part]],
                step_y(2 * part - 1), (self.send_index + part, self.recv_index),
            )

        def last(self, side, part, panel):
            if panel:
                landing = arrived_panel.at[side, self.panel_parts[part]]
            else:
                landing = arrived.at[side, self.parts[part]]
            return copies.make(
                grams.at[k, self.e, self.parts[part]], landing, step_y(2 * side - 1),
                (self.send_index + part, self.recv_index + 2 * side + part),
            )

        def send_last(self, side, part):
            if self.panel is not None:
                self.last(side, part, self.panel).start()
                return

            @pl.when(self.is_panel)
            def _():
                self.last(side, part, True).start()

            @pl.when(jnp.logical_not(self.is_panel))
            def _():
                self.last(side, part, False).start()

        def send_on(self):
            self.join()
            self.send()

        def join(self):
            if not self.panel:

                @pl.when(self.takes)
                def _():
                    self.pair.wait_recv()
                    grams[k, self.e, self.place, :] = grams[k, self.e, self.place, :] + pairs[self.e, self.place, :]

            if self.panel is not False:

                @pl.when(jnp.logical_and(self.holds, jnp.logical_and(self.is_panel, y == 0)))
                def _():
                    rows = pl.ds(self.i * TILE + self.start, self.rows)
                    grams[k, self.e, self.place, :] = grams[k, self.e, self.place, :] + base_ref[rows, :]

        def send(self):
            @self.when(2)
            def _():
                self.relay(0).start()
                self.relay(1).start()

            for side in range(2):

                @self.when(1 + 2 * side)
                def _():
                    self.send_last(side, 1 - side)

        def relay_on(self):
            for side in range(2):

                @self.when(1 + 2 * side)
                def _():
                    part = self.parts[side]
                    self.relay(side).wait_recv()
                    grams[k, self.e, part, :] = grams[k, self.e, part, :] + relays[self.e, part, :]
                    self.send_last(side, side)

        def collect(self):
            @self.when(0)
            def _():
                for side in range(2):
                    for part in (1 - side, side):
                        self.last(side, part, bool(self.panel)).wait_recv()
                if self.panel is None:
                    pl.when(self.is_panel)(lambda: self.add_panel())
                    pl.when(jnp.logical_not(self.is_panel))(lambda: self.add_share())
                elif self.panel:
                    self.add_panel()
                else:
                    self.add_share()

        def add_panel(self):
            rows = pl.ds(self.i * TILE + self.start, self.rows)
            landed = pl.ds(self.start, self.rows)
            panel_ref[2 * c + k, rows, :] = (
                grams[k, self.e, self.place, :] + arrived_panel[0, landed, :] + arrived_panel[1, landed, :]
            )

        def add_share(self):
            done = 0
            while done < self.rows:
                d, start = (self.d * TILE + self.start + done) // TILE, (self.start + done) % TILE
                number = min(self.rows - done, TILE - start)
                rows = pl.ds(wrap(c + OFFSETS[d]) * TILE + start, number)
                place = pl.ds(d * TILE + start, number)
                share_ref[rows, :] = (
                    grams[k, self.e, place, :] + arrived[0, place, :] + arrived[1, place, :] + base_ref[rows, :]
                )
                done += number

        def finish(self):
            if not self.panel:
                pl.when(self.gives)(lambda: self.pair.wait_send())

            @self.when(2)
            def _():
                self.relay(0).wait_send()
                self.relay(1).wait_send()

            for side in range(2):

                @self.when(1 + 2 * side)
                def _():
                    self.last(side, 0, bool(self.panel)).wait_send()
                    self.last(side, 1, bool(self.panel)).wait_send()

    def each(items, name):
        for item in items:
            getattr(item, name)()

    gram_into(0, 0, TILE, 0)
    opening = [Unit(0, 0, (0, 1))]
    each(opening, "send_pair")
    for part in range(TILE // CHUNK):
        start = part * CHUNK
        for step, d, base_slot in streams:
            first_hop[base_slot, d, part].wait_recv()
            if part % 2 == (0 if d == 1 else 1):
                slot = base_slot + (1 if d == -1 else 2)
                copy = copies.make(
                    rows_of(slot, start, CHUNK), rows_of(base_slot + 3, start, CHUNK), step(d), copies.take()
                )
                copy.start()
                second_hop[base_slot, part] = copy
        if part == 0:
            each(opening, "send_on")
        if part == 1:
            halves = []
            for d in (1, 2):
                gram_into(d, 0, HALF, 0)
                halves.append(Unit(d, 0, (0, 1), 0, HALF))
                halves[-1].send_pair()
            for e in (1, 2):
                grams[0, e, pl.ds(0, TILE), :] = gram(0, TILE, column_slots[e], 0, HALF)
                halves.append(Unit(0, e, (0,)))
                halves[-1].send_pair()
            each(opening, "relay_on")
            each(halves, "send_on")
        if part == 2:
            each(halves, "relay_on")

    in_diag = jnp.logical_and(jnp.logical_and(c < 2, y < 2), c <= y)
    diag_z = Spread(copies, step_z, r, in_diag, diag_ref.at[jnp.minimum(y, 1), jnp.minimum(2 * c, 2) + k])
    diag_tiles = ((0, 0), (1, 0), (1, 1))
    diag_y = [Spread(copies, step_y, wrap(y - i), c == t, diag_ref.at[i, 2 * t + k]) for i, t in diag_tiles]
    diag_x = [Spread(copies, step_x, wrap(c - t), jnp.bool_(True), diag_ref.at[i, 2 * t + k]) for i, t in diag_tiles]

    rest = [[], [], []]
    for d in (1, 2):
        gram_into(d, HALF, HALF, 0)
        rest[0].append(Unit(d, 0, (0, 1), HALF, HALF))
        rest[0][-1].send_pair()
    for e in (1, 2):
        grams[1, e, pl.ds(0, TILE), :] = gram(0, TILE, column_slots[e], HALF, HALF)
        product = gram(TILE, 2 * TILE, column_slots[e])
        grams[0, e, pl.ds(TILE, 2 * TILE), :] = product[:, :HALF]
        grams[1, e, pl.ds(TILE, 2 * TILE), :] = product[:, HALF:]
        rest[e] = [Unit(0, e, (1,)), Unit(1, e, (0, 1)), Unit(2, e, (0, 1))]
        each(rest[e], "send_pair")
        each(rest[e - 1], "send_on")
        if e == 2:
            each(rest[0], "relay_on")
    each(rest[2], "send_on")
    each([*opening, *halves, *rest[0]], "collect")

    @pl.when(jnp.logical_and(in_diag, r == 0))
    def _():
        diag_ref[y, 2 * c + k, :, :] = panel_ref[2 * c + k, pl.ds(y * TILE, TILE), :]

    diag_z.start()
    each(rest[1], "relay_on")

    def late_stage(half):
        for base_slot in (0, 3):
            for part in (2 * half, 2 * half + 1):
                second_hop[base_slot, part].wait_recv()
        start = half * HALF
        rows = pl.ds(3 * TILE + start, HALF)
        height = 3 * TILE + start + HALF
        grams[half, 3, pl.ds(0, height), :] = gram(0, height, 6, start, HALF)
        column = [Unit(0, 3, (half,), 0, height, panel=False)]
        each(column, "send_pair")
        for d in range(4):
            column.append(Unit(d, 3, (half,), 0, HALF if d == 3 and half == 0 else TILE, panel=True))
        across = []
        for e in range(3):
            gram_into(3, start, HALF, e)
            across.append(Unit(3, e, (0, 1), start, HALF))
            across[-1].send_pair()
            if e == 1:
                each(column, "send_on")
        if half == 1:
            grams[0, 3, rows, :] = gram(3 * TILE + start, HALF, 6, 0, HALF)
            across.append(Unit(3, 3, (0,), start, HALF))
            across[-1].send_pair()
        each(across, "send_on")
        return [*column, *across]

    first_late = late_stage(0)
    each(rest[2], "relay_on")
    each(first_late, "relay_on")
    second_late = late_stage(1)
    diag_z.forward()
    each(second_late, "relay_on")
    each([*rest[1], *rest[2], *first_late], "collect")
    diag_z.arrive()
    each(diag_y, "start")
    each(second_late, "collect")

    handed = []

    def hand(ref):
        copy = copies.make(ref, ref, sibling, copies.take())
        copy.start()
        handed.append(copy)

    def panel_rows(t, i, start=0, rows=TILE):
        return panel_ref.at[2 * t + k, pl.ds(wrap(i) * TILE + start, rows)]

    panel_x = [
        Spread(copies, step_x, wrap(c - t), jnp.bool_(True), panel_ref.at[2 * t + k, pl.ds(y * TILE, TILE)])
        for t in range(2)
    ]
    each(panel_x, "start")
    has_share = jnp.logical_not(jnp.logical_and(c < 2, y == 0))

    @pl.when(jnp.logical_and(has_share, r == 0))
    def _():
        mirror_ref[...] = share_ref[pl.ds(0, 2 * TILE), :]

    mirror_z = Spread(copies, step_z, r, has_share, mirror_ref)
    mirror_z.start()
    each(diag_y, "forward")
    each(panel_x, "forward")
    each(diag_y, "arrive")
    each(diag_x, "start")
    each(panel_x, "arrive")
    around, again = {}, {}
    for t in range(2):
        for d in (1, -1):
            block = panel_rows(t, y)
            around[t, d] = copies.make(block, block, step_y(d), copies.take())
            around[t, d].start()
        hand(panel_rows(t, y))
    mirror_z.forward()
    each(diag_x, "forward")
    for t in range(2):
        for d, start in ((1, 0), (-1, HALF)):
            around[t, d].wait_recv()
            block = panel_rows(t, y - d, start, HALF)
            again[t, d] = copies.make(block, block, step_y(d), copies.take())
            again[t, d].start()
            hand(panel_rows(t, y - d))
    each(diag_x, "arrive")
    for i, t in diag_tiles:
        hand(diag_ref.at[i, 2 * t + k])
    for t in range(2):
        again[t, 1].wait_recv()
        again[t, -1].wait_recv()
        hand(panel_rows(t, y + 2))
    mirror_z.arrive()
    each(handed, "wait_recv")

    @pl.when(jnp.logical_not(has_share))
    def _():
        block = 2 * jnp.minimum(c, 1) + k
        share_ref[...] = panel_ref[block]
        mirror_ref[pl.ds(TILE, TILE), :] = diag_ref[1, block]

        @pl.when(c == 0)
        def _():
            mirror_ref[pl.ds(0, TILE), :] = diag_ref[0, block]

        @pl.when(c == 1)
        def _():
            for h in range(2):
                mirror_ref[pl.ds(h * HALF, HALF), :] = diag_ref[1, h, pl.ds(k * HALF, HALF), :].T

    for copy in [*first_hop.values(), *second_hop.values(), *around.values(), *again.values(), *handed]:
        copy.wait_send()
    for unit in [*opening, *halves, *rest[0], *rest[1], *rest[2], *first_late, *second_late]:
        unit.finish()
    for spread in [diag_z, *diag_x, *diag_y, *panel_x, mirror_z]:
        spread.finish()


def dot(a, b, contract=(1, 0), precision=HIGHEST):
    return lax.dot_general(
        a, b, (((contract[0],), (contract[1],)), ((), ())),
        precision=precision, preferred_element_type=jnp.float32,
    )


def row_sum_bound(matrix):
    return jnp.max(jnp.sum(jnp.abs(matrix), axis=1, keepdims=True))


def inverse(matrix, x_ref, e_ref):
    size = matrix.shape[0]
    same = lax.broadcasted_iota(jnp.int32, (size, size), 0) == lax.broadcasted_iota(jnp.int32, (size, size), 1)
    identity = jnp.where(same, 1.0, 0.0).astype(jnp.float32)
    diagonal = jnp.where(same, matrix, 0.0)
    across = lax.rsqrt(jnp.sum(diagonal, axis=0, keepdims=True))
    down = lax.rsqrt(jnp.sum(diagonal, axis=1, keepdims=True))
    scaled = matrix * across * down
    alpha = 2.0 / (1.0 + row_sum_bound(scaled))
    start = identity * alpha

    def coarse(x):
        coarse_x = x.astype(jnp.bfloat16)
        gap = identity - dot(scaled.astype(jnp.bfloat16), coarse_x, precision=None)
        return x + dot(coarse_x, gap.astype(jnp.bfloat16), precision=None)

    x_ref[...] = coarse(coarse(start * 2.0 - scaled * (alpha * alpha)))
    gap = identity - dot(scaled, x_ref[...])
    e_ref[...] = gap
    bound = row_sum_bound(gap)

    @pl.when(jnp.logical_not(bound < 0.5))
    def _():
        x_ref[...] = start
        e_ref[...] = identity - dot(scaled, start)

    def more(state):
        count, bound, last = state
        return jnp.logical_and(count < 60, jnp.logical_and(bound > 1e-3, jnp.logical_or(bound > 0.5, bound < last)))

    def step(state):
        count, bound, last = state
        x_ref[...] = x_ref[...] + dot(x_ref[...], e_ref[...])
        gap = identity - dot(scaled, x_ref[...])
        e_ref[...] = gap
        return count + 1, row_sum_bound(gap), bound

    bound = row_sum_bound(e_ref[...])
    lax.while_loop(more, step, (jnp.int32(0), bound, jnp.float32(jnp.inf)))
    x_ref[...] = x_ref[...] + dot(x_ref[...], e_ref[...])
    x_ref[...] = x_ref[...] * across * down


def eliminate_kernel(
    share_in, panel_in, diag_in, mirror_in, schur_out, lower_out,
    share_ref, panel_ref, diag_ref, mirror_ref, schur_ref, lower_ref, x_ref, gap_ref, in_sems, out_sems,
):
    pairs = ((diag_in, diag_ref), (mirror_in, mirror_ref), (panel_in, panel_ref), (share_in, share_ref))
    loads = [pltpu.make_async_copy(src, dst, in_sems.at[n]) for n, (src, dst) in enumerate(pairs)]
    for load in loads:
        load.start()

    def block(i, t):
        return jnp.concatenate([diag_ref[i, 2 * t], diag_ref[i, 2 * t + 1]], axis=1)

    loads[0].wait()
    cross = block(1, 0)
    inverse(block(0, 0), x_ref, gap_ref)
    first = x_ref[...]
    ratio = dot(cross, first)
    inverse(block(1, 1) - dot(ratio, cross, (1, 1)), x_ref, gap_ref)
    second = x_ref[...]
    for load in loads[1:]:
        load.wait()
    above = mirror_ref[:TILE, :]
    below = mirror_ref[TILE:, :] - dot(ratio, above)
    stores = []
    for i in range(4):
        rows = pl.ds(i * TILE, TILE)
        left = jnp.concatenate([panel_ref[0, rows, :], panel_ref[1, rows, :]], axis=1)
        right = jnp.concatenate([panel_ref[2, rows, :], panel_ref[3, rows, :]], axis=1)
        lower_first = dot(left, first)
        lower_second = dot(right - dot(left, ratio, (1, 1)), second)
        lower_ref[rows, :TILE] = lower_first
        lower_ref[rows, TILE:] = lower_second
        schur_ref[rows, :] = share_ref[rows, :] - dot(lower_first, above) - dot(lower_second, below)
        for n, (src, dst) in enumerate(((lower_ref, lower_out), (schur_ref, schur_out))):
            store = pltpu.make_async_copy(src.at[rows], dst.at[rows], out_sems.at[2 * i + n])
            store.start()
            stores.append(store)
    for store in stores:
        store.wait()


def shards(updates, row_mask, base):
    vmem = pl.BlockSpec(memory_space=pltpu.VMEM)
    smem = pl.BlockSpec(memory_space=pltpu.SMEM)
    f32 = jnp.float32
    staged = (
        jax.ShapeDtypeStruct((ROWS, HALF), f32),
        jax.ShapeDtypeStruct((4, ROWS, HALF), f32),
        jax.ShapeDtypeStruct((2, 4, TILE, HALF), f32),
        jax.ShapeDtypeStruct((2 * TILE, HALF), f32),
    )
    between = pl.pallas_call(
        gather_kernel,
        out_shape=staged,
        in_specs=[vmem, smem, vmem],
        out_specs=(vmem,) * 4,
        scratch_shapes=[
            pltpu.VMEM((7 * TILE, DEPTH), jnp.bfloat16),
            pltpu.VMEM((2, 4, ROWS, HALF), f32),
            pltpu.VMEM((4, ROWS, HALF), f32),
            pltpu.VMEM((4, ROWS, HALF), f32),
            pltpu.VMEM((2, ROWS, HALF), f32),
            pltpu.VMEM((2, TILE, HALF), f32),
            pltpu.SemaphoreType.DMA((SENDS,)),
            pltpu.SemaphoreType.DMA((RECEIVES,)),
        ],
        compiler_params=pltpu.CompilerParams(
            collective_id=0, has_side_effects=True, vmem_limit_bytes=56 << 20
        ),
        cost_estimate=pl.CostEstimate(flops=8 << 30, bytes_accessed=8 << 20, transcendentals=0),
    )(updates[0], row_mask, base[:, 0, :])
    result = (jax.ShapeDtypeStruct((ROWS, HALF), f32), jax.ShapeDtypeStruct((ROWS, 2 * TILE), f32))
    anywhere = pl.BlockSpec(memory_space=pl.ANY)
    schur, lower = pl.pallas_call(
        eliminate_kernel,
        out_shape=result,
        in_specs=[anywhere] * 4,
        out_specs=(anywhere,) * 2,
        scratch_shapes=[
            *[pltpu.VMEM(array.shape, f32) for array in (*staged, *result)],
            *[pltpu.VMEM((TILE, TILE), f32)] * 2,
            pltpu.SemaphoreType.DMA((4,)),
            pltpu.SemaphoreType.DMA((8,)),
        ],
        compiler_params=pltpu.CompilerParams(vmem_limit_bytes=60 << 20),
        cost_estimate=pl.CostEstimate(flops=1 << 30, bytes_accessed=8 << 20, transcendentals=0),
    )(*between)
    return schur[:, None, :], lower


def solution(mesh):
    placed = (P("grid", ("prow", "pcol"), None), P("grid", None), P("prow", "pcol", "grid"))
    return jax.shard_map(
        shards,
        mesh=mesh,
        in_specs=placed,
        out_specs=(P("prow", "pcol", "grid"), P("prow", None)),
        check_vma=False,
    )
```

```python
import jax
import jax.numpy as jnp
from jax import lax
from jax.experimental import pallas as pl
from jax.experimental.pallas import tpu as pltpu
from jax.sharding import PartitionSpec as P

TILE = 256
HALF = 128
DEPTH = 4096
ROWS = 1024
CHUNK = 64
SENDS = 165
RECEIVES = 225
MESH = pl.DeviceIdType.MESH
HIGHEST = lax.Precision.HIGHEST
OFFSETS = (0, 1, 3, 2)


def wrap(value):
    return lax.rem(value + 4, 4)


class Copies:
    def __init__(self, send_sems, recv_sems):
        self.send_sems, self.recv_sems, self.sends, self.receives = send_sems, recv_sems, 0, 0

    def take(self, sends=1, receives=1):
        first = self.sends, self.receives
        self.sends, self.receives = self.sends + sends, self.receives + receives
        return first

    def make(self, src, dst, device, index):
        return pltpu.make_async_remote_copy(
            src_ref=src,
            dst_ref=dst,
            send_sem=self.send_sems.at[index[0]],
            recv_sem=self.recv_sems.at[index[1]],
            device_id=device,
            device_id_type=MESH,
        )


class Spread:
    def __init__(self, copies, step, place, holds, block):
        rows = block.shape[0] // 2
        self.place, self.holds = place, holds
        send, receive = copies.take(4, 4)
        halves = [block.at[pl.ds(0, rows)], block.at[pl.ds(rows, rows)]]
        self.up = [copies.make(halves[n], halves[n], step(1), (send + n, receive + n)) for n in (0, 1)]
        self.down = [copies.make(halves[n], halves[n], step(-1), (send + 2 + n, receive + 2 + n)) for n in (1, 0)]

    def when(self, place):
        return pl.when(jnp.logical_and(self.holds, self.place == place))

    def start(self):
        @self.when(0)
        def _():
            for up, down in zip(self.up, self.down):
                up.start()
                down.start()

    def forward(self):
        for place, ways in ((1, self.up), (3, self.down)):

            @self.when(place)
            def _():
                ways[0].wait_recv()
                ways[0].start()

    def arrive(self):
        for place, ways in ((1, self.up), (3, self.down)):

            @self.when(place)
            def _():
                ways[1].wait_recv()

        @self.when(2)
        def _():
            self.up[0].wait_recv()
            self.down[0].wait_recv()

    def finish(self):
        @self.when(0)
        def _():
            for copy in (*self.up, *self.down):
                copy.wait_send()

        for place, ways in ((1, self.up), (3, self.down)):

            @self.when(place)
            def _():
                ways[0].wait_send()


def gather_kernel(
    u_ref, mask_ref, base_ref, share_ref, panel_ref, diag_ref, mirror_ref,
    tiles, grams, pairs, relays, arrived, arrived_panel, send_sems, recv_sems,
):
    grid = lax.axis_index("grid")
    r = lax.axis_index("prow")
    c = lax.axis_index("pcol")
    y, k = grid // 2, lax.rem(grid, 2)
    copies = Copies(send_sems, recv_sems)
    sibling = {"grid": y * 2 + 1 - k}

    def step_x(d):
        return {"pcol": wrap(c + d)}

    def step_y(d):
        return {"grid": wrap(y + d) * 2 + k}

    def step_z(d):
        return {"prow": wrap(r + d)}

    barrier = pltpu.get_barrier_semaphore()
    others = [step_x(1), step_x(-1), step_z(1), step_z(-1), step_y(1), step_y(-1), sibling]
    for other in others:
        pl.semaphore_signal(barrier, inc=1, device_id=other, device_id_type=MESH)
    pl.semaphore_wait(barrier, len(others))

    keep = mask_ref[0, r * 4 + c] > 0
    first_hop, second_hop = {}, {}
    streams = [(step, d, base_slot) for step, base_slot in ((step_x, 0), (step_z, 3)) for d in (-1, 1)]

    def rows_of(slot, start, size):
        return tiles.at[pl.ds(slot * TILE + start, size)]

    for part in range(TILE // CHUNK):
        start = part * CHUNK
        value = u_ref[pl.ds(start, CHUNK), :]
        tiles[pl.ds(start, CHUNK), :] = jnp.where(keep, value, jnp.zeros_like(value))
        for step, d, base_slot in streams:
            slot = base_slot + (1 if d == -1 else 2)
            copy = copies.make(rows_of(0, start, CHUNK), rows_of(slot, start, CHUNK), step(d), copies.take())
            copy.start()
            first_hop[base_slot, d, part] = copy

    def gram(rows_start, rows, slot, columns_start=0, columns=TILE):
        return lax.dot_general(
            tiles[pl.ds(rows_start, rows), :],
            tiles[pl.ds(slot * TILE + columns_start, columns), :],
            (((1,), (1,)), ((), ())),
            preferred_element_type=jnp.float32,
        )

    column_slots = (0, 4, 5, 6)

    def gram_into(d, start, rows, e):
        product = gram(d * TILE + start, rows, column_slots[e])
        place = pl.ds(d * TILE + start, rows)
        grams[0, e, place, :] = product[:, :HALF]
        grams[1, e, place, :] = product[:, HALF:]

    class Unit:
        def __init__(self, d, e, halves, start=0, rows=TILE, panel=None):
            self.d, self.e, self.halves, self.start, self.rows, self.panel = d, e, halves, start, rows, panel
            self.place = pl.ds(d * TILE + start, rows)
            cut = rows // 2
            self.parts = [pl.ds(d * TILE + start + n * cut, cut) for n in range(2)]
            self.panel_parts = [pl.ds(start + n * cut, cut) for n in range(2)]
            self.q = wrap(r + OFFSETS[e])
            self.i = wrap(c + OFFSETS[d])
            self.is_panel = jnp.logical_and(c < 2, self.q == 0)
            self.target = jnp.where(self.is_panel, self.i, self.q)
            self.back = wrap(y - self.target)
            self.pair_index = copies.take(0, 0) if panel else copies.take()
            self.send_index, self.recv_index = copies.take(2, 4)
            if len(halves) == 2:
                self.gives = self.takes = jnp.bool_(True)
            else:
                self.gives, self.takes = k != halves[0], k == halves[0]
            if not panel:
                self.pair = copies.make(
                    grams.at[1 - k, e, self.place], pairs.at[e, self.place], sibling, self.pair_index
                )
            self.holds = self.takes
            if panel is not None:
                self.holds = jnp.logical_and(self.takes, self.is_panel if panel else jnp.logical_not(self.is_panel))

        def send_pair(self):
            pl.when(self.gives)(lambda: self.pair.start())

        def when(self, back):
            return pl.when(jnp.logical_and(self.holds, self.back == back))

        def relay(self, part):
            return copies.make(
                grams.at[k, self.e, self.parts[part]], relays.at[self.e, self.parts[part]],
                step_y(2 * part - 1), (self.send_index + part, self.recv_index),
            )

        def last(self, side, part, panel):
            if panel:
                landing = arrived_panel.at[side, self.panel_parts[part]]
            else:
                landing = arrived.at[side, self.parts[part]]
            return copies.make(
                grams.at[k, self.e, self.parts[part]], landing, step_y(2 * side - 1),
                (self.send_index + part, self.recv_index + 2 * side + part),
            )

        def send_last(self, side, part):
            if self.panel is not None:
                self.last(side, part, self.panel).start()
                return

            @pl.when(self.is_panel)
            def _():
                self.last(side, part, True).start()

            @pl.when(jnp.logical_not(self.is_panel))
            def _():
                self.last(side, part, False).start()

        def send_on(self):
            self.join()
            self.send()

        def join(self):
            if not self.panel:

                @pl.when(self.takes)
                def _():
                    self.pair.wait_recv()
                    grams[k, self.e, self.place, :] = grams[k, self.e, self.place, :] + pairs[self.e, self.place, :]

            if self.panel is not False:

                @pl.when(jnp.logical_and(self.holds, jnp.logical_and(self.is_panel, y == 0)))
                def _():
                    rows = pl.ds(self.i * TILE + self.start, self.rows)
                    grams[k, self.e, self.place, :] = grams[k, self.e, self.place, :] + base_ref[rows, :]

        def send(self):
            @self.when(2)
            def _():
                self.relay(0).start()
                self.relay(1).start()

            for side in range(2):

                @self.when(1 + 2 * side)
                def _():
                    self.send_last(side, 1 - side)

        def relay_on(self):
            for side in range(2):

                @self.when(1 + 2 * side)
                def _():
                    part = self.parts[side]
                    self.relay(side).wait_recv()
                    grams[k, self.e, part, :] = grams[k, self.e, part, :] + relays[self.e, part, :]
                    self.send_last(side, side)

        def collect(self):
            @self.when(0)
            def _():
                for side in range(2):
                    for part in (1 - side, side):
                        self.last(side, part, bool(self.panel)).wait_recv()
                if self.panel is None:
                    pl.when(self.is_panel)(lambda: self.add_panel())
                    pl.when(jnp.logical_not(self.is_panel))(lambda: self.add_share())
                elif self.panel:
                    self.add_panel()
                else:
                    self.add_share()

        def add_panel(self):
            rows = pl.ds(self.i * TILE + self.start, self.rows)
            landed = pl.ds(self.start, self.rows)
            panel_ref[2 * c + k, rows, :] = (
                grams[k, self.e, self.place, :] + arrived_panel[0, landed, :] + arrived_panel[1, landed, :]
            )

        def add_share(self):
            done = 0
            while done < self.rows:
                d, start = (self.d * TILE + self.start + done) // TILE, (self.start + done) % TILE
                number = min(self.rows - done, TILE - start)
                rows = pl.ds(wrap(c + OFFSETS[d]) * TILE + start, number)
                place = pl.ds(d * TILE + start, number)
                share_ref[rows, :] = (
                    grams[k, self.e, place, :] + arrived[0, place, :] + arrived[1, place, :] + base_ref[rows, :]
                )
                done += number

        def finish(self):
            if not self.panel:
                pl.when(self.gives)(lambda: self.pair.wait_send())

            @self.when(2)
            def _():
                self.relay(0).wait_send()
                self.relay(1).wait_send()

            for side in range(2):

                @self.when(1 + 2 * side)
                def _():
                    self.last(side, 0, bool(self.panel)).wait_send()
                    self.last(side, 1, bool(self.panel)).wait_send()

    def each(items, name):
        for item in items:
            getattr(item, name)()

    gram_into(0, 0, TILE, 0)
    opening = [Unit(0, 0, (0, 1))]
    each(opening, "send_pair")
    for part in range(TILE // CHUNK):
        start = part * CHUNK
        for step, d, base_slot in streams:
            first_hop[base_slot, d, part].wait_recv()
            if part % 2 == (0 if d == 1 else 1):
                slot = base_slot + (1 if d == -1 else 2)
                copy = copies.make(
                    rows_of(slot, start, CHUNK), rows_of(base_slot + 3, start, CHUNK), step(d), copies.take()
                )
                copy.start()
                second_hop[base_slot, part] = copy
        if part == 0:
            each(opening, "send_on")
        if part == 1:
            halves = []
            for d in (1, 2):
                gram_into(d, 0, HALF, 0)
                halves.append(Unit(d, 0, (0, 1), 0, HALF))
                halves[-1].send_pair()
            for e in (1, 2):
                grams[0, e, pl.ds(0, TILE), :] = gram(0, TILE, column_slots[e], 0, HALF)
                halves.append(Unit(0, e, (0,)))
                halves[-1].send_pair()
            each(opening, "relay_on")
            each(halves, "send_on")
        if part == 2:
            each(halves, "relay_on")

    in_diag = jnp.logical_and(jnp.logical_and(c < 2, y < 2), c <= y)
    diag_z = Spread(copies, step_z, r, in_diag, diag_ref.at[jnp.minimum(y, 1), jnp.minimum(2 * c, 2) + k])
    diag_tiles = ((0, 0), (1, 0), (1, 1))
    diag_y = [Spread(copies, step_y, wrap(y - i), c == t, diag_ref.at[i, 2 * t + k]) for i, t in diag_tiles]
    diag_x = [Spread(copies, step_x, wrap(c - t), jnp.bool_(True), diag_ref.at[i, 2 * t + k]) for i, t in diag_tiles]

    rest = [[], [], []]
    for d in (1, 2):
        gram_into(d, HALF, HALF, 0)
        rest[0].append(Unit(d, 0, (0, 1), HALF, HALF))
        rest[0][-1].send_pair()
    for e in (1, 2):
        grams[1, e, pl.ds(0, TILE), :] = gram(0, TILE, column_slots[e], HALF, HALF)
        product = gram(TILE, 2 * TILE, column_slots[e])
        grams[0, e, pl.ds(TILE, 2 * TILE), :] = product[:, :HALF]
        grams[1, e, pl.ds(TILE, 2 * TILE), :] = product[:, HALF:]
        rest[e] = [Unit(0, e, (1,)), Unit(1, e, (0, 1)), Unit(2, e, (0, 1))]
        each(rest[e], "send_pair")
        each(rest[e - 1], "send_on")
        if e == 2:
            each(rest[0], "relay_on")
    each(rest[2], "send_on")
    each([*opening, *halves, *rest[0]], "collect")

    @pl.when(jnp.logical_and(in_diag, r == 0))
    def _():
        diag_ref[y, 2 * c + k, :, :] = panel_ref[2 * c + k, pl.ds(y * TILE, TILE), :]

    diag_z.start()
    each(rest[1], "relay_on")

    def late_stage(half):
        for base_slot in (0, 3):
            for part in (2 * half, 2 * half + 1):
                second_hop[base_slot, part].wait_recv()
        start = half * HALF
        rows = pl.ds(3 * TILE + start, HALF)
        height = 3 * TILE + start + HALF
        grams[half, 3, pl.ds(0, height), :] = gram(0, height, 6, start, HALF)
        column = [Unit(0, 3, (half,), 0, height, panel=False)]
        each(column, "send_pair")
        for d in range(4):
            column.append(Unit(d, 3, (half,), 0, HALF if d == 3 and half == 0 else TILE, panel=True))
        across = []
        for e in range(3):
            gram_into(3, start, HALF, e)
            across.append(Unit(3, e, (0, 1), start, HALF))
            across[-1].send_pair()
            if e == 1:
                each(column, "send_on")
        if half == 1:
            grams[0, 3, rows, :] = gram(3 * TILE + start, HALF, 6, 0, HALF)
            across.append(Unit(3, 3, (0,), start, HALF))
            across[-1].send_pair()
        each(across, "send_on")
        return [*column, *across]

    first_late = late_stage(0)
    each(rest[2], "relay_on")
    each(first_late, "relay_on")
    second_late = late_stage(1)
    diag_z.forward()
    each(second_late, "relay_on")
    each([*rest[1], *rest[2], *first_late], "collect")
    diag_z.arrive()
    each(diag_y, "start")
    each(second_late, "collect")

    handed = []

    def hand(ref):
        copy = copies.make(ref, ref, sibling, copies.take())
        copy.start()
        handed.append(copy)

    def panel_rows(t, i, start=0, rows=TILE):
        return panel_ref.at[2 * t + k, pl.ds(wrap(i) * TILE + start, rows)]

    panel_x = [
        Spread(copies, step_x, wrap(c - t), jnp.bool_(True), panel_ref.at[2 * t + k, pl.ds(y * TILE, TILE)])
        for t in range(2)
    ]
    each(panel_x, "start")
    has_share = jnp.logical_not(jnp.logical_and(c < 2, y == 0))

    @pl.when(jnp.logical_and(has_share, r == 0))
    def _():
        mirror_ref[...] = share_ref[pl.ds(0, 2 * TILE), :]

    mirror_z = Spread(copies, step_z, r, has_share, mirror_ref)
    mirror_z.start()
    each(diag_y, "forward")
    each(panel_x, "forward")
    each(diag_y, "arrive")
    each(diag_x, "start")
    each(panel_x, "arrive")
    around, again = {}, {}
    for t in range(2):
        for d in (1, -1):
            block = panel_rows(t, y)
            around[t, d] = copies.make(block, block, step_y(d), copies.take())
            around[t, d].start()
        hand(panel_rows(t, y))
    mirror_z.forward()
    each(diag_x, "forward")
    for t in range(2):
        for d, start in ((1, 0), (-1, HALF)):
            around[t, d].wait_recv()
            block = panel_rows(t, y - d, start, HALF)
            again[t, d] = copies.make(block, block, step_y(d), copies.take())
            again[t, d].start()
            hand(panel_rows(t, y - d))
    each(diag_x, "arrive")
    for i, t in diag_tiles:
        hand(diag_ref.at[i, 2 * t + k])
    for t in range(2):
        again[t, 1].wait_recv()
        again[t, -1].wait_recv()
        hand(panel_rows(t, y + 2))
    mirror_z.arrive()
    each(handed, "wait_recv")

    @pl.when(jnp.logical_not(has_share))
    def _():
        block = 2 * jnp.minimum(c, 1) + k
        share_ref[...] = panel_ref[block]
        mirror_ref[pl.ds(TILE, TILE), :] = diag_ref[1, block]

        @pl.when(c == 0)
        def _():
            mirror_ref[pl.ds(0, TILE), :] = diag_ref[0, block]

        @pl.when(c == 1)
        def _():
            for h in range(2):
                mirror_ref[pl.ds(h * HALF, HALF), :] = diag_ref[1, h, pl.ds(k * HALF, HALF), :].T

    assert (copies.sends, copies.receives) == (SENDS, RECEIVES)
    for copy in [*first_hop.values(), *second_hop.values(), *around.values(), *again.values(), *handed]:
        copy.wait_send()
    for unit in [*opening, *halves, *rest[0], *rest[1], *rest[2], *first_late, *second_late]:
        unit.finish()
    for spread in [diag_z, *diag_x, *diag_y, *panel_x, mirror_z]:
        spread.finish()


def dot(a, b, contract=(1, 0), precision=HIGHEST):
    return lax.dot_general(
        a, b, (((contract[0],), (contract[1],)), ((), ())),
        precision=precision, preferred_element_type=jnp.float32,
    )


def row_sum_bound(matrix):
    return jnp.max(jnp.sum(jnp.abs(matrix), axis=1, keepdims=True))


def inverse(matrix, x_ref, e_ref):
    size = matrix.shape[0]
    same = lax.broadcasted_iota(jnp.int32, (size, size), 0) == lax.broadcasted_iota(jnp.int32, (size, size), 1)
    identity = jnp.where(same, 1.0, 0.0).astype(jnp.float32)
    diagonal = jnp.where(same, matrix, 0.0)
    across = lax.rsqrt(jnp.sum(diagonal, axis=0, keepdims=True))
    down = lax.rsqrt(jnp.sum(diagonal, axis=1, keepdims=True))
    scaled = matrix * across * down
    alpha = 2.0 / (1.0 + row_sum_bound(scaled))
    start = identity * alpha

    def coarse(x):
        coarse_x = x.astype(jnp.bfloat16)
        gap = identity - dot(scaled.astype(jnp.bfloat16), coarse_x, precision=None)
        return x + dot(coarse_x, gap.astype(jnp.bfloat16), precision=None)

    x_ref[...] = coarse(coarse(start * 2.0 - scaled * (alpha * alpha)))
    gap = identity - dot(scaled, x_ref[...])
    x_ref[...] = x_ref[...] + dot(x_ref[...], gap)
    gap = identity - dot(scaled, x_ref[...])
    e_ref[...] = gap
    bound = row_sum_bound(gap)

    @pl.when(jnp.logical_not(bound < 0.5))
    def _():
        x_ref[...] = start
        e_ref[...] = identity - dot(scaled, start)

    def more(state):
        count, bound, last = state
        return jnp.logical_and(count < 60, jnp.logical_and(bound > 1e-3, jnp.logical_or(bound > 0.5, bound < last)))

    def step(state):
        count, bound, last = state
        x_ref[...] = x_ref[...] + dot(x_ref[...], e_ref[...])
        gap = identity - dot(scaled, x_ref[...])
        e_ref[...] = gap
        return count + 1, row_sum_bound(gap), bound

    bound = jnp.where(bound < 0.5, bound, 1.0)
    lax.while_loop(more, step, (jnp.int32(0), bound, jnp.float32(jnp.inf)))
    x_ref[...] = x_ref[...] + dot(x_ref[...], e_ref[...])
    x_ref[...] = x_ref[...] * across * down


def eliminate_kernel(
    share_in, panel_in, diag_in, mirror_in, schur_out, lower_out,
    share_ref, panel_ref, diag_ref, mirror_ref, schur_ref, lower_ref, x_ref, gap_ref, in_sems, out_sems,
):
    pairs = ((diag_in, diag_ref), (mirror_in, mirror_ref), (panel_in, panel_ref), (share_in, share_ref))
    loads = [pltpu.make_async_copy(src, dst, in_sems.at[n]) for n, (src, dst) in enumerate(pairs)]
    for load in loads:
        load.start()

    def block(i, t):
        return jnp.concatenate([diag_ref[i, 2 * t], diag_ref[i, 2 * t + 1]], axis=1)

    loads[0].wait()
    cross = block(1, 0)
    inverse(block(0, 0), x_ref, gap_ref)
    first = x_ref[...]
    ratio = dot(cross, first)
    inverse(block(1, 1) - dot(ratio, cross, (1, 1)), x_ref, gap_ref)
    second = x_ref[...]
    for load in loads[1:]:
        load.wait()
    above = mirror_ref[:TILE, :]
    below = mirror_ref[TILE:, :] - dot(ratio, above)
    stores = []
    for i in range(4):
        rows = pl.ds(i * TILE, TILE)
        left = jnp.concatenate([panel_ref[0, rows, :], panel_ref[1, rows, :]], axis=1)
        right = jnp.concatenate([panel_ref[2, rows, :], panel_ref[3, rows, :]], axis=1)
        lower_first = dot(left, first)
        lower_second = dot(right - dot(left, ratio, (1, 1)), second)
        lower_ref[rows, :TILE] = lower_first
        lower_ref[rows, TILE:] = lower_second
        schur_ref[rows, :] = share_ref[rows, :] - dot(lower_first, above) - dot(lower_second, below)
        for n, (src, dst) in enumerate(((lower_ref, lower_out), (schur_ref, schur_out))):
            store = pltpu.make_async_copy(src.at[rows], dst.at[rows], out_sems.at[2 * i + n])
            store.start()
            stores.append(store)
    for store in stores:
        store.wait()


def shards(updates, row_mask, base):
    vmem = pl.BlockSpec(memory_space=pltpu.VMEM)
    smem = pl.BlockSpec(memory_space=pltpu.SMEM)
    f32 = jnp.float32
    staged = (
        jax.ShapeDtypeStruct((ROWS, HALF), f32),
        jax.ShapeDtypeStruct((4, ROWS, HALF), f32),
        jax.ShapeDtypeStruct((2, 4, TILE, HALF), f32),
        jax.ShapeDtypeStruct((2 * TILE, HALF), f32),
    )
    between = pl.pallas_call(
        gather_kernel,
        out_shape=staged,
        in_specs=[vmem, smem, vmem],
        out_specs=(vmem,) * 4,
        scratch_shapes=[
            pltpu.VMEM((7 * TILE, DEPTH), jnp.bfloat16),
            pltpu.VMEM((2, 4, ROWS, HALF), f32),
            pltpu.VMEM((4, ROWS, HALF), f32),
            pltpu.VMEM((4, ROWS, HALF), f32),
            pltpu.VMEM((2, ROWS, HALF), f32),
            pltpu.VMEM((2, TILE, HALF), f32),
            pltpu.SemaphoreType.DMA((SENDS,)),
            pltpu.SemaphoreType.DMA((RECEIVES,)),
        ],
        compiler_params=pltpu.CompilerParams(
            collective_id=0, has_side_effects=True, vmem_limit_bytes=56 << 20
        ),
        cost_estimate=pl.CostEstimate(flops=8 << 30, bytes_accessed=8 << 20, transcendentals=0),
    )(updates[0], row_mask, base[:, 0, :])
    result = (jax.ShapeDtypeStruct((ROWS, HALF), f32), jax.ShapeDtypeStruct((ROWS, 2 * TILE), f32))
    anywhere = pl.BlockSpec(memory_space=pl.ANY)
    schur, lower = pl.pallas_call(
        eliminate_kernel,
        out_shape=result,
        in_specs=[anywhere] * 4,
        out_specs=(anywhere,) * 2,
        scratch_shapes=[
            *[pltpu.VMEM(array.shape, f32) for array in (*staged, *result)],
            *[pltpu.VMEM((TILE, TILE), f32)] * 2,
            pltpu.SemaphoreType.DMA((4,)),
            pltpu.SemaphoreType.DMA((8,)),
        ],
        compiler_params=pltpu.CompilerParams(vmem_limit_bytes=60 << 20),
        cost_estimate=pl.CostEstimate(flops=1 << 30, bytes_accessed=8 << 20, transcendentals=0),
    )(*between)
    return schur[:, None, :], lower


def solution(mesh):
    placed = (P("grid", ("prow", "pcol"), None), P("grid", None), P("prow", "pcol", "grid"))
    return jax.shard_map(
        shards,
        mesh=mesh,
        in_specs=placed,
        out_specs=(P("prow", "pcol", "grid"), P("prow", None)),
        check_vma=False,
    )
```

```python
import jax
import jax.numpy as jnp
from jax import lax
from jax.experimental import pallas as pl
from jax.experimental.pallas import tpu as pltpu
from jax.sharding import PartitionSpec as P

TILE = 256
HALF = 128
DEPTH = 4096
ROWS = 1024
CHUNK = 64
SENDS = 165
RECEIVES = 225
MESH = pl.DeviceIdType.MESH
HIGHEST = lax.Precision.HIGHEST
OFFSETS = (0, 1, 3, 2)


def wrap(value):
    return lax.rem(value + 4, 4)


class Copies:
    def __init__(self, send_sems, recv_sems):
        self.send_sems, self.recv_sems, self.sends, self.receives = send_sems, recv_sems, 0, 0

    def take(self, sends=1, receives=1):
        first = self.sends, self.receives
        self.sends, self.receives = self.sends + sends, self.receives + receives
        return first

    def make(self, src, dst, device, index):
        return pltpu.make_async_remote_copy(
            src_ref=src,
            dst_ref=dst,
            send_sem=self.send_sems.at[index[0]],
            recv_sem=self.recv_sems.at[index[1]],
            device_id=device,
            device_id_type=MESH,
        )


class Spread:
    def __init__(self, copies, step, place, holds, block):
        rows = block.shape[0] // 2
        self.place, self.holds = place, holds
        send, receive = copies.take(4, 4)
        halves = [block.at[pl.ds(0, rows)], block.at[pl.ds(rows, rows)]]
        self.up = [copies.make(halves[n], halves[n], step(1), (send + n, receive + n)) for n in (0, 1)]
        self.down = [copies.make(halves[n], halves[n], step(-1), (send + 2 + n, receive + 2 + n)) for n in (1, 0)]

    def when(self, place):
        return pl.when(jnp.logical_and(self.holds, self.place == place))

    def start(self):
        @self.when(0)
        def _():
            for up, down in zip(self.up, self.down):
                up.start()
                down.start()

    def forward(self):
        for place, ways in ((1, self.up), (3, self.down)):

            @self.when(place)
            def _():
                ways[0].wait_recv()
                ways[0].start()

    def arrive(self):
        for place, ways in ((1, self.up), (3, self.down)):

            @self.when(place)
            def _():
                ways[1].wait_recv()

        @self.when(2)
        def _():
            self.up[0].wait_recv()
            self.down[0].wait_recv()

    def finish(self):
        @self.when(0)
        def _():
            for copy in (*self.up, *self.down):
                copy.wait_send()

        for place, ways in ((1, self.up), (3, self.down)):

            @self.when(place)
            def _():
                ways[0].wait_send()


def gather_kernel(
    u_ref, mask_ref, base_ref, share_ref, panel_ref, diag_ref, mirror_ref,
    tiles, grams, pairs, relays, arrived, arrived_panel, send_sems, recv_sems,
):
    grid = lax.axis_index("grid")
    r = lax.axis_index("prow")
    c = lax.axis_index("pcol")
    y, k = grid // 2, lax.rem(grid, 2)
    copies = Copies(send_sems, recv_sems)
    sibling = {"grid": y * 2 + 1 - k}

    def step_x(d):
        return {"pcol": wrap(c + d)}

    def step_y(d):
        return {"grid": wrap(y + d) * 2 + k}

    def step_z(d):
        return {"prow": wrap(r + d)}

    barrier = pltpu.get_barrier_semaphore()
    others = [step_x(1), step_x(-1), step_z(1), step_z(-1), step_y(1), step_y(-1), sibling]
    for other in others:
        pl.semaphore_signal(barrier, inc=1, device_id=other, device_id_type=MESH)
    pl.semaphore_wait(barrier, len(others))

    keep = mask_ref[0, r * 4 + c] > 0
    first_hop, second_hop = {}, {}
    streams = [(step, d, base_slot) for step, base_slot in ((step_x, 0), (step_z, 3)) for d in (-1, 1)]

    def rows_of(slot, start, size):
        return tiles.at[pl.ds(slot * TILE + start, size)]

    for part in range(TILE // CHUNK):
        start = part * CHUNK
        value = u_ref[pl.ds(start, CHUNK), :]
        tiles[pl.ds(start, CHUNK), :] = jnp.where(keep, value, jnp.zeros_like(value))
        for step, d, base_slot in streams:
            slot = base_slot + (1 if d == -1 else 2)
            copy = copies.make(rows_of(0, start, CHUNK), rows_of(slot, start, CHUNK), step(d), copies.take())
            copy.start()
            first_hop[base_slot, d, part] = copy

    def gram(rows_start, rows, slot, columns_start=0, columns=TILE):
        return lax.dot_general(
            tiles[pl.ds(rows_start, rows), :],
            tiles[pl.ds(slot * TILE + columns_start, columns), :],
            (((1,), (1,)), ((), ())),
            preferred_element_type=jnp.float32,
        )

    column_slots = (0, 4, 5, 6)

    def gram_into(d, start, rows, e):
        product = gram(d * TILE + start, rows, column_slots[e])
        place = pl.ds(d * TILE + start, rows)
        grams[0, e, place, :] = product[:, :HALF]
        grams[1, e, place, :] = product[:, HALF:]

    class Unit:
        def __init__(self, d, e, halves, start=0, rows=TILE, panel=None):
            self.d, self.e, self.halves, self.start, self.rows, self.panel = d, e, halves, start, rows, panel
            self.place = pl.ds(d * TILE + start, rows)
            cut = rows // 2
            self.parts = [pl.ds(d * TILE + start + n * cut, cut) for n in range(2)]
            self.panel_parts = [pl.ds(start + n * cut, cut) for n in range(2)]
            self.q = wrap(r + OFFSETS[e])
            self.i = wrap(c + OFFSETS[d])
            self.is_panel = jnp.logical_and(c < 2, self.q == 0)
            self.target = jnp.where(self.is_panel, self.i, self.q)
            self.back = wrap(y - self.target)
            self.pair_index = copies.take(0, 0) if panel else copies.take()
            self.send_index, self.recv_index = copies.take(2, 4)
            if len(halves) == 2:
                self.gives = self.takes = jnp.bool_(True)
            else:
                self.gives, self.takes = k != halves[0], k == halves[0]
            if not panel:
                self.pair = copies.make(
                    grams.at[1 - k, e, self.place], pairs.at[e, self.place], sibling, self.pair_index
                )
            self.holds = self.takes
            if panel is not None:
                self.holds = jnp.logical_and(self.takes, self.is_panel if panel else jnp.logical_not(self.is_panel))

        def send_pair(self):
            pl.when(self.gives)(lambda: self.pair.start())

        def when(self, back):
            return pl.when(jnp.logical_and(self.holds, self.back == back))

        def relay(self, part):
            return copies.make(
                grams.at[k, self.e, self.parts[part]], relays.at[self.e, self.parts[part]],
                step_y(2 * part - 1), (self.send_index + part, self.recv_index),
            )

        def last(self, side, part, panel):
            if panel:
                landing = arrived_panel.at[side, self.panel_parts[part]]
            else:
                landing = arrived.at[side, self.parts[part]]
            return copies.make(
                grams.at[k, self.e, self.parts[part]], landing, step_y(2 * side - 1),
                (self.send_index + part, self.recv_index + 2 * side + part),
            )

        def send_last(self, side, part):
            if self.panel is not None:
                self.last(side, part, self.panel).start()
                return

            @pl.when(self.is_panel)
            def _():
                self.last(side, part, True).start()

            @pl.when(jnp.logical_not(self.is_panel))
            def _():
                self.last(side, part, False).start()

        def send_on(self):
            self.join()
            self.send()

        def join(self):
            if not self.panel:

                @pl.when(self.takes)
                def _():
                    self.pair.wait_recv()
                    grams[k, self.e, self.place, :] = grams[k, self.e, self.place, :] + pairs[self.e, self.place, :]

            if self.panel is not False:

                @pl.when(jnp.logical_and(self.holds, jnp.logical_and(self.is_panel, y == 0)))
                def _():
                    rows = pl.ds(self.i * TILE + self.start, self.rows)
                    grams[k, self.e, self.place, :] = grams[k, self.e, self.place, :] + base_ref[rows, :]

        def send(self):
            @self.when(2)
            def _():
                self.relay(0).start()
                self.relay(1).start()

            for side in range(2):

                @self.when(1 + 2 * side)
                def _():
                    self.send_last(side, 1 - side)

        def relay_on(self):
            for side in range(2):

                @self.when(1 + 2 * side)
                def _():
                    part = self.parts[side]
                    self.relay(side).wait_recv()
                    grams[k, self.e, part, :] = grams[k, self.e, part, :] + relays[self.e, part, :]
                    self.send_last(side, side)

        def collect(self):
            @self.when(0)
            def _():
                for side in range(2):
                    for part in (1 - side, side):
                        self.last(side, part, bool(self.panel)).wait_recv()
                if self.panel is None:
                    pl.when(self.is_panel)(lambda: self.add_panel())
                    pl.when(jnp.logical_not(self.is_panel))(lambda: self.add_share())
                elif self.panel:
                    self.add_panel()
                else:
                    self.add_share()

        def add_panel(self):
            rows = pl.ds(self.i * TILE + self.start, self.rows)
            landed = pl.ds(self.start, self.rows)
            panel_ref[2 * c + k, rows, :] = (
                grams[k, self.e, self.place, :] + arrived_panel[0, landed, :] + arrived_panel[1, landed, :]
            )

        def add_share(self):
            done = 0
            while done < self.rows:
                d, start = (self.d * TILE + self.start + done) // TILE, (self.start + done) % TILE
                number = min(self.rows - done, TILE - start)
                rows = pl.ds(wrap(c + OFFSETS[d]) * TILE + start, number)
                place = pl.ds(d * TILE + start, number)
                share_ref[rows, :] = (
                    grams[k, self.e, place, :] + arrived[0, place, :] + arrived[1, place, :] + base_ref[rows, :]
                )
                done += number

        def finish(self):
            if not self.panel:
                pl.when(self.gives)(lambda: self.pair.wait_send())

            @self.when(2)
            def _():
                self.relay(0).wait_send()
                self.relay(1).wait_send()

            for side in range(2):

                @self.when(1 + 2 * side)
                def _():
                    self.last(side, 0, bool(self.panel)).wait_send()
                    self.last(side, 1, bool(self.panel)).wait_send()

    def each(items, name):
        for item in items:
            getattr(item, name)()

    gram_into(0, 0, TILE, 0)
    opening = [Unit(0, 0, (0, 1))]
    each(opening, "send_pair")
    for part in range(TILE // CHUNK):
        start = part * CHUNK
        for step, d, base_slot in streams:
            first_hop[base_slot, d, part].wait_recv()
            if part % 2 == (0 if d == 1 else 1):
                slot = base_slot + (1 if d == -1 else 2)
                copy = copies.make(
                    rows_of(slot, start, CHUNK), rows_of(base_slot + 3, start, CHUNK), step(d), copies.take()
                )
                copy.start()
                second_hop[base_slot, part] = copy
        if part == 0:
            each(opening, "send_on")
        if part == 1:
            halves = []
            for d in (1, 2):
                gram_into(d, 0, HALF, 0)
                halves.append(Unit(d, 0, (0, 1), 0, HALF))
                halves[-1].send_pair()
            for e in (1, 2):
                grams[0, e, pl.ds(0, TILE), :] = gram(0, TILE, column_slots[e], 0, HALF)
                halves.append(Unit(0, e, (0,)))
                halves[-1].send_pair()
            each(opening, "relay_on")
            each(halves, "send_on")
        if part == 2:
            each(halves, "relay_on")

    in_diag = jnp.logical_and(jnp.logical_and(c < 2, y < 2), c <= y)
    diag_z = Spread(copies, step_z, r, in_diag, diag_ref.at[jnp.minimum(y, 1), jnp.minimum(2 * c, 2) + k])
    diag_tiles = ((0, 0), (1, 0), (1, 1))
    diag_y = [Spread(copies, step_y, wrap(y - i), c == t, diag_ref.at[i, 2 * t + k]) for i, t in diag_tiles]
    diag_x = [Spread(copies, step_x, wrap(c - t), jnp.bool_(True), diag_ref.at[i, 2 * t + k]) for i, t in diag_tiles]

    rest = [[], [], []]
    for d in (1, 2):
        gram_into(d, HALF, HALF, 0)
        rest[0].append(Unit(d, 0, (0, 1), HALF, HALF))
        rest[0][-1].send_pair()
    for e in (1, 2):
        grams[1, e, pl.ds(0, TILE), :] = gram(0, TILE, column_slots[e], HALF, HALF)
        product = gram(TILE, 2 * TILE, column_slots[e])
        grams[0, e, pl.ds(TILE, 2 * TILE), :] = product[:, :HALF]
        grams[1, e, pl.ds(TILE, 2 * TILE), :] = product[:, HALF:]
        rest[e] = [Unit(0, e, (1,)), Unit(1, e, (0, 1)), Unit(2, e, (0, 1))]
        each(rest[e], "send_pair")
        each(rest[e - 1], "send_on")
        if e == 2:
            each(rest[0], "relay_on")
    each(rest[2], "send_on")
    each([*opening, *halves, *rest[0]], "collect")

    @pl.when(jnp.logical_and(in_diag, r == 0))
    def _():
        diag_ref[y, 2 * c + k, :, :] = panel_ref[2 * c + k, pl.ds(y * TILE, TILE), :]

    diag_z.start()
    each(rest[1], "relay_on")

    def late_stage(half):
        for base_slot in (0, 3):
            for part in (2 * half, 2 * half + 1):
                second_hop[base_slot, part].wait_recv()
        start = half * HALF
        rows = pl.ds(3 * TILE + start, HALF)
        height = 3 * TILE + start + HALF
        grams[half, 3, pl.ds(0, height), :] = gram(0, height, 6, start, HALF)
        column = [Unit(0, 3, (half,), 0, height, panel=False)]
        each(column, "send_pair")
        for d in range(4):
            column.append(Unit(d, 3, (half,), 0, HALF if d == 3 and half == 0 else TILE, panel=True))
        across = []
        for e in range(3):
            gram_into(3, start, HALF, e)
            across.append(Unit(3, e, (0, 1), start, HALF))
            across[-1].send_pair()
            if e == 1:
                each(column, "send_on")
        if half == 1:
            grams[0, 3, rows, :] = gram(3 * TILE + start, HALF, 6, 0, HALF)
            across.append(Unit(3, 3, (0,), start, HALF))
            across[-1].send_pair()
        each(across, "send_on")
        return [*column, *across]

    first_late = late_stage(0)
    each(rest[2], "relay_on")
    each(first_late, "relay_on")
    second_late = late_stage(1)
    diag_z.forward()
    each(second_late, "relay_on")
    each([*rest[1], *rest[2], *first_late], "collect")
    diag_z.arrive()
    each(diag_y, "start")
    each(second_late, "collect")

    handed = []

    def hand(ref):
        copy = copies.make(ref, ref, sibling, copies.take())
        copy.start()
        handed.append(copy)

    def panel_rows(t, i, start=0, rows=TILE):
        return panel_ref.at[2 * t + k, pl.ds(wrap(i) * TILE + start, rows)]

    panel_x = [
        Spread(copies, step_x, wrap(c - t), jnp.bool_(True), panel_ref.at[2 * t + k, pl.ds(y * TILE, TILE)])
        for t in range(2)
    ]
    each(panel_x, "start")
    has_share = jnp.logical_not(jnp.logical_and(c < 2, y == 0))

    @pl.when(jnp.logical_and(has_share, r == 0))
    def _():
        mirror_ref[...] = share_ref[pl.ds(0, 2 * TILE), :]

    mirror_z = Spread(copies, step_z, r, has_share, mirror_ref)
    mirror_z.start()
    each(diag_y, "forward")
    each(panel_x, "forward")
    each(diag_y, "arrive")
    each(diag_x, "start")
    each(panel_x, "arrive")
    around, again = {}, {}
    for t in range(2):
        for d in (1, -1):
            block = panel_rows(t, y)
            around[t, d] = copies.make(block, block, step_y(d), copies.take())
            around[t, d].start()
        hand(panel_rows(t, y))
    mirror_z.forward()
    each(diag_x, "forward")
    for t in range(2):
        for d, start in ((1, 0), (-1, HALF)):
            around[t, d].wait_recv()
            block = panel_rows(t, y - d, start, HALF)
            again[t, d] = copies.make(block, block, step_y(d), copies.take())
            again[t, d].start()
            hand(panel_rows(t, y - d))
    each(diag_x, "arrive")
    for i, t in diag_tiles:
        hand(diag_ref.at[i, 2 * t + k])
    for t in range(2):
        again[t, 1].wait_recv()
        again[t, -1].wait_recv()
        hand(panel_rows(t, y + 2))
    mirror_z.arrive()
    each(handed, "wait_recv")

    @pl.when(jnp.logical_not(has_share))
    def _():
        block = 2 * jnp.minimum(c, 1) + k
        share_ref[...] = panel_ref[block]
        mirror_ref[pl.ds(TILE, TILE), :] = diag_ref[1, block]

        @pl.when(c == 0)
        def _():
            mirror_ref[pl.ds(0, TILE), :] = diag_ref[0, block]

        @pl.when(c == 1)
        def _():
            for h in range(2):
                mirror_ref[pl.ds(h * HALF, HALF), :] = diag_ref[1, h, pl.ds(k * HALF, HALF), :].T

    assert (copies.sends, copies.receives) == (SENDS, RECEIVES)
    for copy in [*first_hop.values(), *second_hop.values(), *around.values(), *again.values(), *handed]:
        copy.wait_send()
    for unit in [*opening, *halves, *rest[0], *rest[1], *rest[2], *first_late, *second_late]:
        unit.finish()
    for spread in [diag_z, *diag_x, *diag_y, *panel_x, mirror_z]:
        spread.finish()


def dot(a, b, contract=(1, 0), precision=HIGHEST):
    return lax.dot_general(
        a, b, (((contract[0],), (contract[1],)), ((), ())),
        precision=precision, preferred_element_type=jnp.float32,
    )


def row_sum_bound(matrix):
    return jnp.max(jnp.sum(jnp.abs(matrix), axis=1, keepdims=True))


def inverse(matrix, x_ref, e_ref):
    size = matrix.shape[0]
    same = lax.broadcasted_iota(jnp.int32, (size, size), 0) == lax.broadcasted_iota(jnp.int32, (size, size), 1)
    identity = jnp.where(same, 1.0, 0.0).astype(jnp.float32)
    diagonal = jnp.where(same, matrix, 0.0)
    across = lax.rsqrt(jnp.sum(diagonal, axis=0, keepdims=True))
    down = lax.rsqrt(jnp.sum(diagonal, axis=1, keepdims=True))
    scaled = matrix * across * down
    alpha = 2.0 / (1.0 + row_sum_bound(scaled))
    start = identity * alpha

    def coarse(x):
        coarse_x = x.astype(jnp.bfloat16)
        gap = identity - dot(scaled.astype(jnp.bfloat16), coarse_x, precision=None)
        return x + dot(coarse_x, gap.astype(jnp.bfloat16), precision=None)

    x_ref[...] = coarse(coarse(start * 2.0 - scaled * (alpha * alpha)))
    gap = identity - dot(scaled, x_ref[...])
    x_ref[...] = x_ref[...] + dot(x_ref[...], gap)
    gap = identity - dot(scaled, x_ref[...])
    e_ref[...] = gap
    bound = row_sum_bound(gap)

    @pl.when(jnp.logical_not(bound < 0.5))
    def _():
        x_ref[...] = start
        e_ref[...] = identity - dot(scaled, start)

    def more(state):
        count, bound, last = state
        return jnp.logical_and(count < 60, jnp.logical_and(bound > 1e-3, jnp.logical_or(bound > 0.5, bound < last)))

    def step(state):
        count, bound, last = state
        x_ref[...] = x_ref[...] + dot(x_ref[...], e_ref[...])
        gap = identity - dot(scaled, x_ref[...])
        e_ref[...] = gap
        return count + 1, row_sum_bound(gap), bound

    bound = jnp.where(bound < 0.5, bound, 1.0)
    lax.while_loop(more, step, (jnp.int32(0), bound, jnp.float32(jnp.inf)))
    x_ref[...] = x_ref[...] + dot(x_ref[...], e_ref[...])
    x_ref[...] = x_ref[...] * across * down


def eliminate_kernel(
    share_in, panel_in, diag_in, mirror_in, schur_out, lower_out,
    share_ref, panel_ref, diag_ref, mirror_ref, schur_ref, lower_ref, x_ref, gap_ref, in_sems, out_sems,
):
    pairs = ((diag_in, diag_ref), (mirror_in, mirror_ref), (panel_in, panel_ref), (share_in, share_ref))
    loads = [pltpu.make_async_copy(src, dst, in_sems.at[n]) for n, (src, dst) in enumerate(pairs)]
    for load in loads:
        load.start()

    def block(i, t):
        return jnp.concatenate([diag_ref[i, 2 * t], diag_ref[i, 2 * t + 1]], axis=1)

    loads[0].wait()
    cross = block(1, 0)
    head = block(0, 0)
    inverse(head, x_ref, gap_ref)
    first = x_ref[...]
    loads[1].wait()
    sides = jnp.concatenate([cross.T, mirror_ref[:TILE, :]], axis=1)
    solved = dot(first, sides)
    solved = solved + dot(first, sides - dot(head, solved))
    ratio, above = solved[:, :TILE], solved[:, TILE:]
    rest = block(1, 1) - dot(cross, ratio)
    inverse(rest, x_ref, gap_ref)
    second = x_ref[...]
    target = mirror_ref[TILE:, :] - dot(cross, above)
    below = dot(second, target)
    below = below + dot(second, target - dot(rest, below))
    for load in loads[2:]:
        load.wait()
    stores = []
    for i in range(4):
        rows = pl.ds(i * TILE, TILE)
        left = jnp.concatenate([panel_ref[0, rows, :], panel_ref[1, rows, :]], axis=1)
        right = jnp.concatenate([panel_ref[2, rows, :], panel_ref[3, rows, :]], axis=1)
        lower_first = dot(left, first)
        right = right - dot(left, ratio)
        lower_second = dot(right, second)
        lower_ref[rows, :TILE] = lower_first
        lower_ref[rows, TILE:] = lower_second
        schur_ref[rows, :] = share_ref[rows, :] - dot(left, above) - dot(right, below)
        for n, (src, dst) in enumerate(((lower_ref, lower_out), (schur_ref, schur_out))):
            store = pltpu.make_async_copy(src.at[rows], dst.at[rows], out_sems.at[2 * i + n])
            store.start()
            stores.append(store)
    for store in stores:
        store.wait()


def shards(updates, row_mask, base):
    vmem = pl.BlockSpec(memory_space=pltpu.VMEM)
    smem = pl.BlockSpec(memory_space=pltpu.SMEM)
    f32 = jnp.float32
    staged = (
        jax.ShapeDtypeStruct((ROWS, HALF), f32),
        jax.ShapeDtypeStruct((4, ROWS, HALF), f32),
        jax.ShapeDtypeStruct((2, 4, TILE, HALF), f32),
        jax.ShapeDtypeStruct((2 * TILE, HALF), f32),
    )
    between = pl.pallas_call(
        gather_kernel,
        out_shape=staged,
        in_specs=[vmem, smem, vmem],
        out_specs=(vmem,) * 4,
        scratch_shapes=[
            pltpu.VMEM((7 * TILE, DEPTH), jnp.bfloat16),
            pltpu.VMEM((2, 4, ROWS, HALF), f32),
            pltpu.VMEM((4, ROWS, HALF), f32),
            pltpu.VMEM((4, ROWS, HALF), f32),
            pltpu.VMEM((2, ROWS, HALF), f32),
            pltpu.VMEM((2, TILE, HALF), f32),
            pltpu.SemaphoreType.DMA((SENDS,)),
            pltpu.SemaphoreType.DMA((RECEIVES,)),
        ],
        compiler_params=pltpu.CompilerParams(
            collective_id=0, has_side_effects=True, vmem_limit_bytes=56 << 20
        ),
        cost_estimate=pl.CostEstimate(flops=8 << 30, bytes_accessed=8 << 20, transcendentals=0),
    )(updates[0], row_mask, base[:, 0, :])
    result = (jax.ShapeDtypeStruct((ROWS, HALF), f32), jax.ShapeDtypeStruct((ROWS, 2 * TILE), f32))
    anywhere = pl.BlockSpec(memory_space=pl.ANY)
    schur, lower = pl.pallas_call(
        eliminate_kernel,
        out_shape=result,
        in_specs=[anywhere] * 4,
        out_specs=(anywhere,) * 2,
        scratch_shapes=[
            *[pltpu.VMEM(array.shape, f32) for array in (*staged, *result)],
            *[pltpu.VMEM((TILE, TILE), f32)] * 2,
            pltpu.SemaphoreType.DMA((4,)),
            pltpu.SemaphoreType.DMA((8,)),
        ],
        compiler_params=pltpu.CompilerParams(vmem_limit_bytes=60 << 20),
        cost_estimate=pl.CostEstimate(flops=1 << 30, bytes_accessed=8 << 20, transcendentals=0),
    )(*between)
    return schur[:, None, :], lower


def solution(mesh):
    placed = (P("grid", ("prow", "pcol"), None), P("grid", None), P("prow", "pcol", "grid"))
    return jax.shard_map(
        shards,
        mesh=mesh,
        in_specs=placed,
        out_specs=(P("prow", "pcol", "grid"), P("prow", None)),
        check_vma=False,
    )
```
